256 devices in a mesh: depth: 16 (over x_lo, y, core), dp: 16 (over x_hi, z).
Axes of the slice: x: 4 (x_hi: 2, x_lo: 2; x = x_hi * 2 + x_lo), y: 4, z: 8, core: 2. Of those that a mesh axis runs over, the one named last changes fastest.
Arguments:
- token_ids: int32 [2048], P('dp'), may hold values from 0 to 20479
- embedding: bfloat16 [20480, 512], P('depth'), may hold values from -6 to 6
- w_up: bfloat16 [32, 512, 2048], P('depth'), may hold values from -0.25 to 0.25
- w_down: bfloat16 [32, 2048, 512], P('depth'), may hold values from -0.125 to 0.125
- cotangent: bfloat16 [2048, 512], P('dp'), may hold values from -0.119628906 to 0.119628906
Outputs:
- grad_up: float32 [32, 512, 2048], P('depth', 'dp')
- grad_down: float32 [32, 2048, 512], P('depth', 'dp')
The draws below stay inside these ranges and needn't reach their ends.
All inputs are finite; a program needn't handle non-finite values.
Results may differ from the reference program's by a relative error of at most 0.03.
Values may be sent and summed in bfloat16 or wider, within the bound.
A program may use at most 64 MiB of HBM per device.

```python
import jax
import jax.numpy as jnp
from jax import lax

D = 512
FF = 2048
L_DEV = 2
RELAX = 3
LAYERS = 32
VOCAB = 20480
TOKENS = 2048
N_DEPTH = 16


def set_ends(entries, rng, least, high):
    place = [jax.random.randint(jax.random.fold_in(rng, axis), (), 0, length) for axis, length in enumerate(entries.shape)]
    longest = entries.shape.index(max(entries.shape))
    next_to = place[:longest] + [(place[longest] + 1) % entries.shape[longest]] + place[longest + 1:]
    return entries.at[tuple(place)].set(least).at[tuple(next_to)].set(high)


def shard_levels(own_key, dims, pieces, low, top_value):
    loudness, own = 1.0, jax.random.fold_in(own_key, 6)
    for dim, parts in pieces:
        draws = jnp.exp(jax.random.uniform(jax.random.fold_in(own, dim), (parts,), jnp.float32, low / len(pieces), top_value / len(pieces)))
        loudness = loudness * jnp.repeat(draws, dims[dim] // parts).reshape([-1 if axis == dim else 1 for axis in range(len(dims))])
    return loudness


def normal_values(key, dims, width, reach, split=(), kind=jnp.bfloat16):
    values = jax.random.normal(key, dims, jnp.float32) * width
    if len(split) > 0:
        values = shard_levels(key, dims, split, -0.22, 0.18) * values
    return jnp.clip(values, min=-reach, max=reach).astype(kind)


def setup_inputs(seed: int = 0) -> dict:
    streams_of = jax.random.split(jax.random.key(seed), 6)
    token_ids = set_ends(jax.random.randint(streams_of[0], (TOKENS,), 0, VOCAB), jax.random.fold_in(streams_of[0], 1), 0, VOCAB - 1).astype(jnp.int32)
    embedding = normal_values(streams_of[1], (VOCAB, D), 1.0, 6.0, ((0, 16),))
    w_up = normal_values(streams_of[2], (LAYERS, D, FF), D ** -0.5, 0.25, ((0, 16),))
    w_down = normal_values(streams_of[3], (LAYERS, FF, D), FF ** -0.5, 0.125, ((0, 16),))
    cotangent = normal_values(streams_of[4], (TOKENS, D), 0.02, 0.119628906, ((0, 16),))
    return {"token_ids": token_ids, "embedding": embedding, "w_up": w_up, "w_down": w_down, "cotangent": cotangent}


EPSILON = 1e-06
GAMMA = 0.05

def layer_forward(state, weight_up, weight_down):
    scale = lax.rsqrt(lax.optimization_barrier(jnp.mean(state * state, axis=-1, keepdims=True)) + EPSILON)
    normed = (state * scale).astype(jnp.bfloat16)
    before = jnp.dot(normed, weight_up, preferred_element_type=jnp.float32)
    hidden = jax.nn.silu(before).astype(jnp.bfloat16)
    output = state + jnp.dot(hidden, weight_down, preferred_element_type=jnp.float32)
    return (output, (scale, normed, before, hidden))

def layer_adjoint(state, saved, adjoint, weight_up, weight_down):
    scale, normed, before, hidden = saved
    adjoint_low = adjoint.astype(jnp.bfloat16)
    toward_hidden = lax.dot_general(adjoint_low, weight_down, (((1,), (1,)), ((), ())), preferred_element_type=jnp.float32)
    sigma = jax.nn.sigmoid(before)
    delta = (toward_hidden * sigma * (1.0 + before * (1.0 - sigma))).astype(jnp.bfloat16)
    toward_normed = lax.dot_general(delta, weight_up, (((1,), (1,)), ((), ())), preferred_element_type=jnp.float32)
    unit = state * scale
    inner = lax.optimization_barrier(jnp.mean(toward_normed * unit, axis=-1, keepdims=True))
    return (adjoint + scale * (toward_normed - unit * inner), adjoint_low, delta)

def coarse_matrix(weight_up, weight_down):
    total = jnp.dot(weight_up[0], weight_down[0], preferred_element_type=jnp.float32)
    for layer in range(1, weight_up.shape[0]):
        total = total + jnp.dot(weight_up[layer], weight_down[layer], preferred_element_type=jnp.float32)
    return jnp.eye(weight_up.shape[1], dtype=jnp.float32) + GAMMA * total

def block_forward(packed):
    state, ups, downs = packed
    for layer in range(L_DEV):
        state, unused = layer_forward(state, ups[layer], downs[layer])
    return state

def block_states(packed):
    state, ups, downs = packed
    inputs = []
    for layer in range(L_DEV):
        inputs.append(state)
        state, unused = layer_forward(state, ups[layer], downs[layer])
    return jnp.stack(inputs, 0)

def block_adjoint(packed):
    adjoint, states, ups, downs = packed
    for layer in reversed(range(L_DEV)):
        unused, saved = layer_forward(states[layer], ups[layer], downs[layer])
        adjoint, low, delta = layer_adjoint(states[layer], saved, adjoint, ups[layer], downs[layer])
    return adjoint

def block_grads(packed):
    adjoint, states, ups, downs = packed
    grads_up = [None] * L_DEV
    grads_down = [None] * L_DEV
    for layer in reversed(range(L_DEV)):
        unused, saved = layer_forward(states[layer], ups[layer], downs[layer])
        scale, normed, before, hidden = saved
        adjoint, low, delta = layer_adjoint(states[layer], saved, adjoint, ups[layer], downs[layer])
        grads_down[layer] = lax.dot_general(hidden, low, (((0,), (0,)), ((), ())), preferred_element_type=jnp.float32)
        grads_up[layer] = lax.dot_general(normed, delta, (((0,), (0,)), ((), ())), preferred_element_type=jnp.float32)
    return (jnp.stack(grads_up, 0), jnp.stack(grads_down, 0))

def project(packed):
    return jnp.dot(packed[0], packed[1], precision=lax.Precision.HIGHEST)

def forward_link(carry, packed):
    matrix, rest = packed
    carry = jnp.dot(carry, matrix, precision=lax.Precision.HIGHEST) + rest
    return (carry, carry)

def reference(token_ids, embedding, w_up, w_down, cotangent):
    start = jnp.take(embedding, token_ids, axis=0).astype(jnp.float32)
    ups = w_up.reshape(N_DEPTH, L_DEV, D, FF)
    downs = w_down.reshape(N_DEPTH, L_DEV, FF, D)
    matrices = lax.map(lambda packed: coarse_matrix(packed[0], packed[1]), (ups, downs))
    transposed = jnp.swapaxes(matrices, 1, 2)
    zeros = jnp.zeros_like(start)
    coarse = jnp.broadcast_to(start[None], (N_DEPTH,) + start.shape)
    previous = coarse
    for sweep in range(RELAX):
        ends = lax.map(block_forward, (coarse, ups, downs))
        previous = coarse
        coarse = jnp.concatenate([start[None], ends[:-1]], 0)
    projected = lax.map(project, (previous, matrices))
    tau = coarse - jnp.concatenate([zeros[None], projected[:-1]], 0)
    unused, carried = lax.scan(forward_link, tau[0], (matrices[:-1], tau[1:]))
    corrected = jnp.concatenate([tau[:1], carried], 0)
    states = lax.map(block_states, (corrected, ups, downs))
    final = cotangent.astype(jnp.float32)
    adjoints = jnp.broadcast_to(final[None], (N_DEPTH,) + final.shape)
    before = adjoints
    for sweep in range(RELAX):
        begins = lax.map(block_adjoint, (adjoints, states, ups, downs))
        before = adjoints
        adjoints = jnp.concatenate([begins[1:], final[None]], 0)
    back_projected = lax.map(project, (before, transposed))
    back_tau = adjoints - jnp.concatenate([back_projected[1:], zeros[None]], 0)
    unused, back_carried = lax.scan(forward_link, back_tau[-1], (transposed[1:], back_tau[:-1]), reverse=True)
    adjoint_corrected = jnp.concatenate([back_carried, back_tau[-1:]], 0)
    grad_up, grad_down = lax.map(block_grads, (adjoint_corrected, states, ups, downs))
    return (grad_up.reshape(N_DEPTH * L_DEV, D, FF), grad_down.reshape(N_DEPTH * L_DEV, FF, D))
```

```python
import functools

import jax
import jax.numpy as jnp
from jax import lax
from jax.experimental import pallas as pl
from jax.experimental.pallas import tpu as pltpu
from jax.sharding import PartitionSpec as P

RELAX = 3
EPSILON = 1e-06
GAMMA = 0.05
F32, BF16 = jnp.float32, jnp.bfloat16
MESH = pl.DeviceIdType.MESH


def nn(a, b):
    return jnp.dot(a, b, preferred_element_type=F32)


def nt(a, b):
    return lax.dot_general(a, b, (((1,), (1,)), ((), ())), preferred_element_type=F32)


def sigmoid(p):
    return 0.5 * jnp.tanh(0.5 * p) + 0.5


def kernel(
    nd, nz,
    tok, emb, wu_hbm, wd_hbm, cot,
    gu_out, gd_out,
    wu, wd,
    epick, erecv, estart,
    own_d, pair_d, all_n,
    cbuf, fsend, abuf, asend,
    tsend, tpair, usend, ubuf, ysend, ybuf,
    bsend, bpair, wsend, wbuf, zsend, zbuf,
    corr, unit, scales, slope,
    rbuf, wus, wds, norm_t, hid_t, slope_s,
    gu, gd, gus, gds, gurecv, gdrecv,
    load_sem, e_s, e_r, e2_s, e2_r, d_s, d_r, n_s, n_r,
    f_s, f_r, a_s, a_r, t_s, t_r, u_s, u_r, y_s, y_r,
    b_s, b_r, w_s, w_r, z_s, z_r, ring_s, ring_r, g_s, g_r, h_s, h_r,
):
    T, D = cot.shape
    L, _, FF = wu.shape
    ndp, nchip = 2 * nz, nd // 2
    k, p = lax.axis_index("depth"), lax.axis_index("dp")
    core, chip = k % 2, k // 2
    x, z = p // nz, p % nz
    F = FF // ndp
    vocab = emb.shape[0]
    wide = min(512, FF)

    def remote(src, dst, ssem, rsem, depth=k, dp=p):
        return pltpu.make_async_remote_copy(
            src_ref=src, dst_ref=dst, send_sem=ssem, recv_sem=rsem,
            device_id={"depth": depth, "dp": dp}, device_id_type=MESH,
        )

    load_up = pltpu.make_async_copy(wu_hbm, wu, load_sem.at[0])
    load_down = pltpu.make_async_copy(wd_hbm, wd, load_sem.at[1])
    load_up.start()
    load_down.start()

    barrier = pltpu.get_barrier_semaphore()

    def greet_depth(i, c):
        pl.semaphore_signal(barrier, inc=1, device_id={"depth": (k + i) % nd, "dp": p}, device_id_type=MESH)
        return c

    def greet_dp(i, c):
        pl.semaphore_signal(barrier, inc=1, device_id={"depth": k, "dp": (p + i) % ndp}, device_id_type=MESH)
        return c

    lax.fori_loop(1, nd, greet_depth, 0)
    lax.fori_loop(1, ndp, greet_dp, 0)

    R, H = T // nchip, D // 2
    local = tok[...] - k * vocab
    onehot = (local == lax.broadcasted_iota(jnp.int32, (T, vocab), 1)).astype(BF16)
    picked = nn(onehot, emb[...]).astype(BF16)
    for c in range(nd):
        epick[c] = picked[(c // 2) * R:(c // 2 + 1) * R, (c % 2) * H:(c % 2 + 1) * H]
    pl.semaphore_wait(barrier, nd + ndp - 2)

    def pick_copy(i):
        t = (k + i) % nd
        return remote(epick.at[t], erecv.at[k], e_s.at[i], e_r.at[k], depth=t)

    def pick_arrival(i):
        t = (k + i) % nd
        return remote(epick.at[t], erecv.at[t], e_s.at[i], e_r.at[t], depth=t)

    def start_copy(i):
        t = (k + i) % nd
        return remote(estart.at[k], estart.at[k], e2_s.at[i], e2_r.at[k], depth=t)

    def start_arrival(i):
        t = (k + i) % nd
        return remote(estart.at[t], estart.at[t], e2_s.at[i], e2_r.at[t], depth=t)

    def each(low, high, f):
        def body(i, c):
            f(i)
            return c
        lax.fori_loop(low, high, body, 0)

    each(1, nd, lambda i: pick_copy(i).start())
    erecv[k] = epick[k]

    load_up.wait()
    load_down.wait()

    def coarse_rows(i):
        rows = pl.ds(pl.multiple_of(i * 128, 128), 128)
        total = nn(wu[0, rows, :], wd[0])
        total = total + nn(wu[1, rows, :], wd[1])
        own_d[rows, :] = (GAMMA * total).astype(BF16)

    each(0, D // 128, coarse_rows)
    d_copy = remote(own_d, pair_d, d_s, d_r, depth=k + 1 - 2 * core)
    d_copy.start()

    each(1, nd, lambda i: pick_arrival(i).wait_recv())
    total = erecv[0].astype(F32)
    for c in range(1, nd):
        total = total + erecv[c].astype(F32)
    estart[k] = total.astype(BF16)
    each(1, nd, lambda i: start_copy(i).start())

    d_copy.wait_recv()

    def n_copy(i):
        t = (chip + i) % nchip
        return remote(all_n.at[chip], all_n.at[chip], n_s.at[i], n_r.at[chip], depth=2 * t)

    def n_arrival(i):
        t = (chip + i) % nchip
        return remote(all_n.at[t], all_n.at[t], n_s.at[i], n_r.at[t], depth=2 * t)

    @pl.when(core == 0)
    def _():
        product = nn(own_d[...], pair_d[...])
        all_n[chip] = (product + own_d[...].astype(F32) + pair_d[...].astype(F32)).astype(BF16)
        each(1, nchip, lambda i: n_copy(i).start())

    for half in range(2):
        at = pl.multiple_of(half * (FF // 2) + z * F, 128)
        for layer in range(L):
            wus[layer, :, half * F:(half + 1) * F] = wu[layer, :, pl.ds(at, F)]
            wds[layer, half * F:(half + 1) * F, :] = wd[layer, pl.ds(at, F), :]

    each(1, nd, lambda i: start_arrival(i).wait_recv())
    for c in range(nd):
        cbuf[0, (c // 2) * R:(c // 2 + 1) * R, (c % 2) * H:(c % 2 + 1) * H] = estart[c].astype(F32)

    def forward(v, layer, save):
        scale = lax.rsqrt(jnp.mean(v * v, axis=-1, keepdims=True) + EPSILON)
        n = v * scale
        normed = n.astype(BF16)
        if save:
            unit[layer] = n
            scales[layer] = scale
            rbuf[layer, z] = normed
        total = None
        for at in range(0, FF, wide):
            pre = nn(normed, wu[layer, :, at:at + wide])
            s = sigmoid(pre)
            if save:
                slope[layer, :, at:at + wide] = s * (1.0 + pre * (1.0 - s))
            part = nn((pre * s).astype(BF16), wd[layer, at:at + wide, :])
            total = part if total is None else total + part
        return v + total

    def adjoint(g, layer):
        low = g.astype(BF16)
        q = None
        for at in range(0, FF, wide):
            toward = nt(low, wd[layer, at:at + wide, :])
            delta = (toward * slope[layer, :, at:at + wide]).astype(BF16)
            part = nt(delta, wu[layer, :, at:at + wide])
            q = part if q is None else q + part
        n = unit[layer]
        inner = jnp.mean(q * n, axis=-1, keepdims=True)
        return g + scales[layer] * (q - n * inner)

    def f_copy(s):
        return remote(fsend.at[s], cbuf.at[s + 1], f_s.at[s], f_r.at[s], depth=(k + 1) % nd)

    def forward_sweep(s):
        v = cbuf[s]
        for layer in range(L):
            v = forward(v, layer, False)
        fsend[s] = v

        @pl.when(k < nd - 1)
        def _():
            f_copy(s).start()

        @pl.when(k > 0)
        def _():
            f_copy(s).wait_recv()

        @pl.when(k == 0)
        def _():
            cbuf[s + 1] = cbuf[0]

    each(0, RELAX, forward_sweep)

    def times(v, d):
        return v + nn(v.astype(BF16), d)

    def times_t(v, d):
        return v + nt(v.astype(BF16), d)

    t_copy = remote(tsend, tpair, t_s, t_r, depth=k + 1 - 2 * core)

    def u_copy(c):
        return remote(usend.at[pl.ds(c * R, R)], ubuf.at[chip], u_s.at[c], u_r.at[chip], depth=2 * c)

    def u_arrival(c):
        return remote(usend.at[pl.ds(c * R, R)], ubuf.at[c], u_s.at[c], u_r.at[c], depth=2 * c)

    def y_copy(src, dst, ss, rs, c, to):
        return remote(src.at[c], dst.at[pl.ds(pl.multiple_of(chip * R, R), R)], ss.at[c, to], rs.at[chip], depth=2 * c + to)

    def y_arrival(src, dst, ss, rs, c):
        return remote(src.at[c], dst.at[pl.ds(c * R, R)], ss.at[c, 0], rs.at[c], depth=2 * c)

    def give(src, dst, ss, rs, c):
        y_copy(src, dst, ss, rs, c, 1).start()

        @pl.when(chip != c)
        def _():
            y_copy(src, dst, ss, rs, c, 0).start()

        @pl.when(chip == c)
        def _():
            dst[pl.ds(pl.multiple_of(chip * R, R), R), :] = src[c]

    def take(src, dst, ss, rs):
        for c in range(nchip):
            @pl.when((core == 1) | (chip != c))
            def _(c=c):
                y_arrival(src, dst, ss, rs, c).wait_recv()

    change = cbuf[RELAX] - cbuf[RELAX - 1]

    @pl.when(core == 0)
    def _():
        tsend[...] = times(change, own_d[...]).astype(BF16)
        t_copy.start()
        each(1, nchip, lambda i: n_arrival(i).wait_recv())
        for c in range(nchip):
            u_arrival(c).wait_recv()
        y = jnp.zeros((R, D), F32)
        for c in range(nchip):
            ysend[c] = y.astype(BF16)
            give(ysend, ybuf, y_s, y_r, c)
            if c < nchip - 1:
                y = times(y, all_n[c]) + ubuf[c].astype(F32)
        take(ysend, ybuf, y_s, y_r)
        corr[...] = cbuf[RELAX] + ybuf[...].astype(F32)

    @pl.when(core == 1)
    def _():
        t_copy.wait_recv()
        usend[...] = times(change + tpair[...].astype(F32), own_d[...]).astype(BF16)
        for c in range(nchip):
            u_copy(c).start()
        take(ysend, ybuf, y_s, y_r)
        corr[...] = (
            cbuf[RELAX] + tpair[...].astype(F32) + times(ybuf[...].astype(F32), pair_d[...])
        )

    steps = ((nz // 2, nz - 1 - nz // 2), (nz - 1 - nz // 2, nz // 2))
    most = nz // 2

    def ring_copy(r, way, s):
        slot = (z - s + nz) % nz if way == 0 else (z + s) % nz
        to = (z + 1) % nz if way == 0 else (z + nz - 1) % nz
        return remote(rbuf.at[r, slot], rbuf.at[r, slot], ring_s.at[r, way, s], ring_r.at[r, way, s], dp=x * nz + to)

    def ring_slot(way, s):
        return (z - s - 1 + nz) % nz if way == 0 else (z + s + 1) % nz

    def ring_arrival(r, way, s):
        slot = ring_slot(way, s)
        to = (z + 1) % nz if way == 0 else (z + nz - 1) % nz
        return remote(rbuf.at[r, slot], rbuf.at[r, slot], ring_s.at[r, way, s], ring_r.at[r, way, s], dp=x * nz + to)

    def ring_begin(r):
        for way in range(2):
            if steps[r % 2][way] > 0:
                ring_copy(r, way, 0).start()

    def ring_step(r, s):
        for way in range(2):
            if s < steps[r % 2][way]:
                ring_arrival(r, way, s).wait_recv()
                if s + 1 < steps[r % 2][way]:
                    ring_copy(r, way, s + 1).start()

    def ring_end(r):
        for way in range(2):
            for s in range(steps[r % 2][way]):
                ring_copy(r, way, s).wait_send()

    v = corr[...]
    for layer in range(L):
        v = forward(v, layer, True)
        ring_begin(layer)

    def a_copy(s):
        return remote(asend.at[s], abuf.at[s + 1], a_s.at[s], a_r.at[s], depth=(k + nd - 1) % nd)

    abuf[0] = cot[...]

    for s in range(RELAX):
        g = abuf[s].astype(F32)
        for layer in reversed(range(L)):
            g = adjoint(g, layer)
        asend[s] = g.astype(BF16)

        @pl.when(k > 0)
        def _():
            a_copy(s).start()

        if s < most:
            ring_step(0, s)
            ring_step(1, s)

        @pl.when(k < nd - 1)
        def _():
            a_copy(s).wait_recv()

        @pl.when(k == nd - 1)
        def _():
            abuf[s + 1] = abuf[0]

    b_copy = remote(bsend, bpair, b_s, b_r, depth=k + 1 - 2 * core)

    def w_copy(c):
        return remote(wsend.at[pl.ds(c * R, R)], wbuf.at[chip], w_s.at[c], w_r.at[chip], depth=2 * c)

    def w_arrival(c):
        return remote(wsend.at[pl.ds(c * R, R)], wbuf.at[c], w_s.at[c], w_r.at[c], depth=2 * c)

    change = abuf[RELAX].astype(F32) - abuf[RELAX - 1].astype(F32)

    @pl.when(core == 1)
    def _():
        bsend[...] = times_t(change, own_d[...]).astype(BF16)
        b_copy.start()

    for s in range(RELAX, most):
        ring_step(0, s)
        ring_step(1, s)

    def prepare(j):
        for layer in range(L):
            normed = rbuf[layer, j]
            norm_t[layer, j] = normed.T
            pre = nn(normed, wus[layer])
            s = sigmoid(pre)
            hid_t[layer, j] = (pre * s).astype(BF16).T
            slope_s[layer, j] = s * (1.0 + pre * (1.0 - s))

    @pl.when(core == 0)
    def _():
        b_copy.wait_recv()
        wsend[...] = times_t(change + bpair[...].astype(F32), own_d[...]).astype(BF16)
        for c in range(nchip):
            @pl.when(chip != c)
            def _(c=c):
                w_copy(c).start()

            @pl.when(chip == c)
            def _(c=c):
                wbuf[c] = wsend[c * R:(c + 1) * R, :]

        for c in range(nchip):
            @pl.when(chip != c)
            def _(c=c):
                w_arrival(c).wait_recv()
        y = jnp.zeros((R, D), F32)
        for c in reversed(range(nchip)):
            zsend[c] = y.astype(BF16)
            give(zsend, zbuf, z_s, z_r, c)
            if c > 0:
                y = times_t(y, all_n[c]) + wbuf[c].astype(F32)

    each(0, nz, prepare)

    @pl.when(core == 0)
    def _():
        take(zsend, zbuf, z_s, z_r)
        corr[...] = (
            abuf[RELAX].astype(F32) + bpair[...].astype(F32) + times_t(zbuf[...].astype(F32), pair_d[...])
        )

    @pl.when(core == 1)
    def _():
        take(zsend, zbuf, z_s, z_r)
        corr[...] = abuf[RELAX].astype(F32) + zbuf[...].astype(F32)

    g = corr[...]
    rbuf[L + 1, z] = g.astype(BF16)
    ring_begin(L + 1)
    g = adjoint(g, 1)
    rbuf[L, z] = g.astype(BF16)
    ring_begin(L)

    gu[...] = jnp.zeros_like(gu)
    gd[...] = jnp.zeros_like(gd)

    def contract(layer, j):
        low = rbuf[L + layer, j]
        delta = (nt(low, wds[layer]) * slope_s[layer, j]).astype(BF16)
        gu[layer] += nn(norm_t[layer, j], delta)
        gd[layer] += nn(hid_t[layer, j], low)

    contract(1, z)
    contract(0, z)
    for s in range(most):
        for layer in (1, 0):
            ring_step(L + layer, s)
        for layer in (1, 0):
            for way in range(2):
                if s < steps[layer][way]:
                    contract(layer, ring_slot(way, s))

    rows = D // ndp

    def g_copy(layer, i):
        t = (p + i) % ndp
        return remote(
            gus.at[layer, pl.ds(pl.multiple_of(t * rows, rows), rows)], gurecv.at[layer, p],
            g_s.at[layer, i], g_r.at[layer, p], dp=t,
        )

    def g_arrival(layer, i):
        t = (p + i) % ndp
        return remote(
            gus.at[layer, pl.ds(pl.multiple_of(t * rows, rows), rows)], gurecv.at[layer, t],
            g_s.at[layer, i], g_r.at[layer, t], dp=t,
        )

    def h_copy(layer):
        return remote(
            gds.at[layer, pl.ds(pl.multiple_of((1 - x) * F, F), F)], gdrecv.at[layer],
            h_s.at[layer], h_r.at[layer], dp=(1 - x) * nz + z,
        )

    for layer in (1, 0):
        gus[layer] = gu[layer].astype(BF16)
        each(1, ndp, lambda i: g_copy(layer, i).start())
        gds[layer] = gd[layer].astype(BF16)
        h_copy(layer).start()
        gurecv[layer, p] = gus[layer, pl.ds(pl.multiple_of(p * rows, rows), rows), :]

    for layer in (1, 0):
        h_copy(layer).wait_recv()
        gd_out[layer] = gd[layer, pl.ds(pl.multiple_of(x * F, F), F), :] + gdrecv[layer].astype(F32)
        each(1, ndp, lambda i: g_arrival(layer, i).wait_recv())
        for j in range(nz):
            both = gurecv[layer, j].astype(F32) + gurecv[layer, nz + j].astype(F32)
            gu_out[layer, :, j * F:(j + 1) * F] = both[:, :F]
            gu_out[layer, :, FF // 2 + j * F:FF // 2 + (j + 1) * F] = both[:, F:]

    each(1, nd, lambda i: pick_copy(i).wait_send())
    each(1, nd, lambda i: start_copy(i).wait_send())
    d_copy.wait_send()

    @pl.when(k < nd - 1)
    def _():
        each(0, RELAX, lambda s: f_copy(s).wait_send())

    @pl.when(k > 0)
    def _():
        each(0, RELAX, lambda s: a_copy(s).wait_send())

    @pl.when(core == 0)
    def _():
        each(1, nchip, lambda i: n_copy(i).wait_send())
        t_copy.wait_send()
        for src, dst, ss, rs in ((ysend, ybuf, y_s, y_r), (zsend, zbuf, z_s, z_r)):
            for c in range(nchip):
                y_copy(src, dst, ss, rs, c, 1).wait_send()

                @pl.when(chip != c)
                def _():
                    y_copy(src, dst, ss, rs, c, 0).wait_send()

        for c in range(nchip):
            @pl.when(chip != c)
            def _():
                w_copy(c).wait_send()

    @pl.when(core == 1)
    def _():
        b_copy.wait_send()
        for c in range(nchip):
            u_copy(c).wait_send()

    for r in range(2 * L):
        ring_end(r)
    for layer in range(L):
        each(1, ndp, lambda i: g_copy(layer, i).wait_send())
        h_copy(layer).wait_send()


def shards(nd, ndp, token_ids, embedding, w_up, w_down, cotangent):
    T, D = cotangent.shape
    L, _, FF = w_up.shape
    nz, nchip = ndp // 2, nd // 2
    R, F = T // nchip, FF // ndp
    most = max(nz // 2, 1)
    V = pltpu.VMEM
    sem = pltpu.SemaphoreType.DMA
    scratch = [
        V((L, D, FF), BF16), V((L, FF, D), BF16),
        V((nd, R, D // 2), BF16), V((nd, R, D // 2), BF16), V((nd, R, D // 2), BF16),
        V((D, D), BF16), V((D, D), BF16), V((nchip, D, D), BF16),
        V((RELAX + 1, T, D), F32), V((RELAX, T, D), F32), V((RELAX + 1, T, D), BF16), V((RELAX, T, D), BF16),
        V((T, D), BF16), V((T, D), BF16), V((T, D), BF16), V((nchip, R, D), BF16), V((nchip, R, D), BF16), V((T, D), BF16),
        V((T, D), BF16), V((T, D), BF16), V((T, D), BF16), V((nchip, R, D), BF16), V((nchip, R, D), BF16), V((T, D), BF16),
        V((T, D), F32), V((L, T, D), F32), V((L, T, 1), F32), V((L, T, FF), F32),
        V((2 * L, nz, T, D), BF16), V((L, D, 2 * F), BF16), V((L, 2 * F, D), BF16),
        V((L, nz, D, T), BF16), V((L, nz, 2 * F, T), BF16), V((L, nz, T, 2 * F), F32),
        V((L, D, 2 * F), F32), V((L, 2 * F, D), F32), V((L, D, 2 * F), BF16), V((L, 2 * F, D), BF16),
        V((L, ndp, D // ndp, 2 * F), BF16), V((L, F, D), BF16),
        sem((2,)), sem((nd,)), sem((nd,)), sem((nd,)), sem((nd,)), sem, sem, sem((nchip,)), sem((nchip,)),
        sem((RELAX,)), sem((RELAX,)), sem((RELAX,)), sem((RELAX,)),
        sem, sem, sem((nchip,)), sem((nchip,)), sem((nchip, 2)), sem((nchip,)),
        sem, sem, sem((nchip,)), sem((nchip,)), sem((nchip, 2)), sem((nchip,)),
        sem((2 * L, 2, most)), sem((2 * L, 2, most)), sem((L, ndp)), sem((L, ndp)), sem((L,)), sem((L,)),
    ]
    vmem = pl.BlockSpec(memory_space=pltpu.VMEM)
    hbm = pl.BlockSpec(memory_space=pl.ANY)
    return pl.pallas_call(
        functools.partial(kernel, nd, nz),
        out_shape=(
            jax.ShapeDtypeStruct((L, D // ndp, FF), F32),
            jax.ShapeDtypeStruct((L, FF // ndp, D), F32),
        ),
        in_specs=[vmem, vmem, hbm, hbm, vmem],
        out_specs=(vmem, vmem),
        scratch_shapes=scratch,
        compiler_params=pltpu.CompilerParams(
            collective_id=0, has_side_effects=True, vmem_limit_bytes=58 * 1024 * 1024
        ),
    )(token_ids[:, None], embedding, w_up, w_down, cotangent)


def solution(mesh):
    in_specs = (
        P("dp"),
        P("depth", None),
        P("depth", None, None),
        P("depth", None, None),
        P("dp", None),
    )
    out_specs = (P("depth", "dp", None), P("depth", "dp", None))
    body = functools.partial(shards, mesh.shape["depth"], mesh.shape["dp"])
    return jax.shard_map(body, mesh=mesh, in_specs=in_specs, out_specs=out_specs, check_vma=False)
```

```python
import functools

import jax
import jax.numpy as jnp
from jax import lax
from jax.experimental import pallas as pl
from jax.experimental.pallas import tpu as pltpu
from jax.sharding import PartitionSpec as P

RELAX = 3
EPSILON = 1e-06
GAMMA = 0.05
F32, BF16 = jnp.float32, jnp.bfloat16
MESH = pl.DeviceIdType.MESH


def nn(a, b):
    return jnp.dot(a, b, preferred_element_type=F32)


def nt(a, b):
    return lax.dot_general(a, b, (((1,), (1,)), ((), ())), preferred_element_type=F32)


def sigmoid(p):
    return 0.5 * jnp.tanh(0.5 * p) + 0.5


def kernel(
    nd, nz,
    tok, emb_hbm, wu_hbm, wd_hbm, cot,
    gu_out, gd_out,
    wu, wd, emb,
    epick, erecv, estart,
    own_d, pair_d, all_n,
    cbuf, fsend, abuf, asend,
    tsend, tpair, usend, ubuf, ysend, ybuf,
    bsend, bpair, wsend, wbuf, zsend, zbuf,
    corr, unit, scales, slope,
    rbuf, wus, wds, norm_t, hid_t, slope_s,
    gu, gd, gus, gds, gurecv, gdrecv, gx, gsum, csend, crecv,
    load_sem, e_s, e_r, e2_s, e2_r, d_s, d_r, n_s, n_r,
    f_s, f_r, a_s, a_r, t_s, t_r, u_s, u_r, y_s, y_r,
    b_s, b_r, w_s, w_r, z_s, z_r, ring_s, ring_r, g_s, g_r, h_s, h_r, x_s, x_r, c_s, c_r,
):
    T, D = cot.shape
    L, _, FF = wu.shape
    ndp, nchip = 2 * nz, nd // 2
    k, p = lax.axis_index("depth"), lax.axis_index("dp")
    core, chip = k % 2, k // 2
    span = max(nchip // 2, 1)
    half, lane = chip // span, chip % span
    Q = T // span
    x, z = p // nz, p % nz
    F = FF // ndp
    vocab = emb.shape[0]
    wide = min(512, FF)

    def remote(src, dst, ssem, rsem, depth=k, dp=p):
        return pltpu.make_async_remote_copy(
            src_ref=src, dst_ref=dst, send_sem=ssem, recv_sem=rsem,
            device_id={"depth": depth, "dp": dp}, device_id_type=MESH,
        )

    load_up = pltpu.make_async_copy(wu_hbm, wu, load_sem.at[0])
    load_down = pltpu.make_async_copy(wd_hbm, wd, load_sem.at[1])
    load_rows = pltpu.make_async_copy(emb_hbm, emb, load_sem.at[2])
    load_rows.start()
    load_up.start()
    load_down.start()

    barrier = pltpu.get_barrier_semaphore()
    pending = []

    def greet_depth(i, c):
        pl.semaphore_signal(barrier, inc=1, device_id={"depth": (k + i) % nd, "dp": p}, device_id_type=MESH)
        return c

    def greet_dp(i, c):
        pl.semaphore_signal(barrier, inc=1, device_id={"depth": k, "dp": (p + i) % ndp}, device_id_type=MESH)
        return c

    lax.fori_loop(1, nd, greet_depth, 0)
    lax.fori_loop(1, ndp, greet_dp, 0)

    R, H = T // nchip, D // 2
    load_rows.wait()
    local = jnp.broadcast_to(tok[...] - k * vocab, (T, T)).T[:, :1]
    onehot = (local == lax.broadcasted_iota(jnp.int32, (T, vocab), 1)).astype(BF16)
    picked = nn(onehot, emb[...]).astype(BF16)
    for c in range(nd):
        epick[c] = picked[(c // 2) * R:(c // 2 + 1) * R, (c % 2) * H:(c % 2 + 1) * H]
    pl.semaphore_wait(barrier, nd + ndp - 2)

    def pick_copy(i):
        t = (k + i) % nd
        return remote(epick.at[t], erecv.at[k], e_s.at[i], e_r.at[k], depth=t)

    def pick_arrival(i):
        t = (k + i) % nd
        return remote(epick.at[t], erecv.at[t], e_s.at[i], e_r.at[t], depth=t)

    def start_copy(i):
        t = (k + i) % nd
        return remote(estart.at[k], estart.at[k], e2_s.at[i], e2_r.at[k], depth=t)

    def start_arrival(i):
        t = (k + i) % nd
        return remote(estart.at[t], estart.at[t], e2_s.at[i], e2_r.at[t], depth=t)

    def each(low, high, f):
        def body(i, c):
            f(i)
            return c
        lax.fori_loop(low, high, body, 0)

    each(1, nd, lambda i: pick_copy(i).start())
    pending.append(lambda: each(1, nd, lambda i: pick_copy(i).wait_send()))
    erecv[k] = epick[k]

    load_up.wait()
    load_down.wait()

    def coarse_rows(i):
        rows = pl.ds(pl.multiple_of(i * 128, 128), 128)
        total = nn(wu[0, rows, :], wd[0])
        total = total + nn(wu[1, rows, :], wd[1])
        own_d[rows, :] = (GAMMA * total).astype(BF16)

    each(0, D // 128, coarse_rows)
    d_copy = remote(own_d, pair_d, d_s, d_r, depth=k + 1 - 2 * core)
    d_copy.start()
    pending.append(d_copy.wait_send)

    each(1, nd, lambda i: pick_arrival(i).wait_recv())
    total = erecv[0].astype(F32)
    for c in range(1, nd):
        total = total + erecv[c].astype(F32)
    estart[k] = total.astype(BF16)
    each(1, nd, lambda i: start_copy(i).start())
    pending.append(lambda: each(1, nd, lambda i: start_copy(i).wait_send()))

    d_copy.wait_recv()

    def n_copy(i):
        t = (lane + i) % span
        return remote(all_n.at[lane], all_n.at[lane], n_s.at[i], n_r.at[lane], depth=2 * (half * span + t))

    def n_arrival(i):
        t = (lane + i) % span
        return remote(all_n.at[t], all_n.at[t], n_s.at[i], n_r.at[t], depth=2 * (half * span + t))

    @pl.when(core == 0)
    def _():
        product = nn(own_d[...], pair_d[...])
        all_n[lane] = (product + own_d[...].astype(F32) + pair_d[...].astype(F32)).astype(BF16)
        each(1, span, lambda i: n_copy(i).start())

    def on(condition, f):
        pending.append(lambda: pl.when(condition)(f))

    on(core == 0, lambda: each(1, span, lambda i: n_copy(i).wait_send()))

    for piece in range(2):
        at = pl.multiple_of(piece * (FF // 2) + z * F, 128)
        for layer in range(L):
            wus[layer, :, piece * F:(piece + 1) * F] = wu[layer, :, pl.ds(at, F)]
            wds[layer, piece * F:(piece + 1) * F, :] = wd[layer, pl.ds(at, F), :]

    each(1, nd, lambda i: start_arrival(i).wait_recv())
    for c in range(nd):
        cbuf[0, (c // 2) * R:(c // 2 + 1) * R, (c % 2) * H:(c % 2 + 1) * H] = estart[c]

    def forward(v, layer, save):
        scale = lax.rsqrt(jnp.mean(v * v, axis=-1, keepdims=True) + EPSILON)
        n = v * scale
        normed = n.astype(BF16)
        if save:
            unit[layer] = n
            scales[layer] = scale
            rbuf[layer, z] = normed
        total = None
        for at in range(0, FF, wide):
            pre = nn(normed, wu[layer, :, at:at + wide])
            s = sigmoid(pre)
            if save:
                slope[layer, :, at:at + wide] = s * (1.0 + pre * (1.0 - s))
            part = nn((pre * s).astype(BF16), wd[layer, at:at + wide, :])
            total = part if total is None else total + part
        return v + total

    def adjoint(g, layer):
        low = g.astype(BF16)
        q = None
        for at in range(0, FF, wide):
            toward = nt(low, wd[layer, at:at + wide, :])
            delta = (toward * slope[layer, :, at:at + wide]).astype(BF16)
            part = nt(delta, wu[layer, :, at:at + wide])
            q = part if q is None else q + part
        n = unit[layer]
        inner = jnp.mean(q * n, axis=-1, keepdims=True)
        return g + scales[layer] * (q - n * inner)

    def f_copy(s):
        return remote(fsend.at[s], cbuf.at[s + 1], f_s.at[s], f_r.at[s], depth=(k + 1) % nd)

    def forward_sweep(s):
        v = cbuf[s].astype(F32)
        for layer in range(L):
            v = forward(v, layer, False)
        fsend[s] = v.astype(BF16)

        @pl.when(k < nd - 1)
        def _():
            f_copy(s).start()

        @pl.when(k > 0)
        def _():
            f_copy(s).wait_recv()

        @pl.when(k == 0)
        def _():
            cbuf[s + 1] = cbuf[0]

    each(0, RELAX, forward_sweep)
    on(k < nd - 1, lambda: each(0, RELAX, lambda s: f_copy(s).wait_send()))

    def times(v, d):
        return v + nn(v.astype(BF16), d)

    def times_t(v, d):
        return v + nt(v.astype(BF16), d)

    t_copy = remote(tsend, tpair, t_s, t_r, depth=k + 1 - 2 * core)

    def rows_of(c):
        return pl.ds(c * Q, Q)

    def u_copy(c):
        return remote(usend.at[rows_of(c)], ubuf.at[lane], u_s.at[c], u_r.at[lane], depth=2 * (half * span + c))

    def u_arrival(c):
        return remote(usend.at[rows_of(c)], ubuf.at[c], u_s.at[c], u_r.at[c], depth=2 * (half * span + c))

    mine = pl.ds(pl.multiple_of(lane * Q, Q), Q)

    def y_copy(src, dst, ss, rs, c, to):
        return remote(src.at[c], dst.at[mine], ss.at[c, to], rs.at[lane], depth=2 * (half * span + c) + to)

    def y_arrival(src, dst, ss, rs, c):
        return remote(src.at[c], dst.at[rows_of(c)], ss.at[c, 0], rs.at[c], depth=2 * (half * span + c))

    def give(src, dst, ss, rs, c):
        y_copy(src, dst, ss, rs, c, 1).start()

        @pl.when(lane != c)
        def _():
            y_copy(src, dst, ss, rs, c, 0).start()

        @pl.when(lane == c)
        def _():
            dst[mine, :] = src[c]

    def take(src, dst, ss, rs):
        for c in range(span):
            @pl.when((core == 1) | (lane != c))
            def _(c=c):
                y_arrival(src, dst, ss, rs, c).wait_recv()

    across = (k + nchip) % nd
    c_copy = remote(csend.at[0], crecv.at[0], c_s.at[0], c_r.at[0], depth=across)
    c_back = remote(csend.at[1], crecv.at[1], c_s.at[1], c_r.at[1], depth=across)

    change = cbuf[RELAX].astype(F32) - cbuf[RELAX - 1].astype(F32)

    @pl.when(core == 0)
    def _():
        tsend[...] = times(change, own_d[...]).astype(BF16)
        t_copy.start()
        each(1, span, lambda i: n_arrival(i).wait_recv())
        for c in range(span):
            u_arrival(c).wait_recv()

        @pl.when(half == 0)
        def _():
            crecv[0] = jnp.zeros((Q, D), BF16)

        @pl.when(half == 1)
        def _():
            c_copy.wait_recv()

        y = crecv[0].astype(F32)
        for c in range(span):
            ysend[c] = y.astype(BF16)
            give(ysend, ybuf, y_s, y_r, c)
            y = times(y, all_n[c]) + ubuf[c].astype(F32)

        @pl.when(half == 0)
        def _():
            csend[0] = y.astype(BF16)
            c_copy.start()

        take(ysend, ybuf, y_s, y_r)
        corr[...] = cbuf[RELAX].astype(F32) + ybuf[...].astype(F32)

    @pl.when(core == 1)
    def _():
        t_copy.wait_recv()
        usend[...] = times(change + tpair[...].astype(F32), own_d[...]).astype(BF16)
        for c in range(span):
            u_copy(c).start()
        take(ysend, ybuf, y_s, y_r)
        corr[...] = (
            cbuf[RELAX].astype(F32) + tpair[...].astype(F32) + times(ybuf[...].astype(F32), pair_d[...])
        )

    def given(src, dst, ss, rs):
        for c in range(span):
            y_copy(src, dst, ss, rs, c, 1).wait_send()
            pl.when(lane != c)(y_copy(src, dst, ss, rs, c, 0).wait_send)

    def scan_sent():
        t_copy.wait_send()
        given(ysend, ybuf, y_s, y_r)
        pl.when(half == 0)(c_copy.wait_send)

    def u_sent():
        for c in range(span):
            u_copy(c).wait_send()

    on(core == 0, scan_sent)
    on(core == 1, u_sent)

    steps = ((nz // 2, nz - 1 - nz // 2), (nz - 1 - nz // 2, nz // 2))
    most = nz // 2

    def ring_copy(r, way, s):
        slot = (z - s + nz) % nz if way == 0 else (z + s) % nz
        to = (z + 1) % nz if way == 0 else (z + nz - 1) % nz
        return remote(rbuf.at[r, slot], rbuf.at[r, slot], ring_s.at[r, way, s], ring_r.at[r, way, s], dp=x * nz + to)

    def ring_slot(way, s):
        return (z - s - 1 + nz) % nz if way == 0 else (z + s + 1) % nz

    def ring_arrival(r, way, s):
        slot = ring_slot(way, s)
        to = (z + 1) % nz if way == 0 else (z + nz - 1) % nz
        return remote(rbuf.at[r, slot], rbuf.at[r, slot], ring_s.at[r, way, s], ring_r.at[r, way, s], dp=x * nz + to)

    def ring_begin(r):
        pending.append(lambda: ring_end(r))
        for way in range(2):
            if steps[r % 2][way] > 0:
                ring_copy(r, way, 0).start()

    def ring_step(r, s):
        for way in range(2):
            if s < steps[r % 2][way]:
                ring_arrival(r, way, s).wait_recv()
                if s + 1 < steps[r % 2][way]:
                    ring_copy(r, way, s + 1).start()

    def ring_end(r):
        for way in range(2):
            for s in range(steps[r % 2][way]):
                ring_copy(r, way, s).wait_send()

    def prepare(layer, j):
        normed = rbuf[layer, j]
        norm_t[layer, j] = normed.T
        pre = nn(normed, wus[layer])
        s = sigmoid(pre)
        hid_t[layer, j] = (pre * s).astype(BF16).T
        slope_s[layer, j] = s * (1.0 + pre * (1.0 - s))

    def gather_step(s):
        for layer in range(L):
            ring_step(layer, s)
        for layer in range(L):
            for way in range(2):
                if s < steps[layer][way]:
                    prepare(layer, ring_slot(way, s))

    v = corr[...]
    for layer in range(L):
        v = forward(v, layer, True)
        ring_begin(layer)

    def a_copy(s):
        return remote(asend.at[s], abuf.at[s + 1], a_s.at[s], a_r.at[s], depth=(k + nd - 1) % nd)

    abuf[0] = cot[...]

    for s in range(RELAX):
        g = abuf[s].astype(F32)
        for layer in reversed(range(L)):
            g = adjoint(g, layer)
        asend[s] = g.astype(BF16)

        @pl.when(k > 0)
        def _():
            a_copy(s).start()

        if s == 0:
            prepare(0, z)
            prepare(1, z)
        if s < most:
            gather_step(s)

        @pl.when(k < nd - 1)
        def _():
            a_copy(s).wait_recv()

        @pl.when(k == nd - 1)
        def _():
            abuf[s + 1] = abuf[0]

    on(k > 0, lambda: each(0, RELAX, lambda s: a_copy(s).wait_send()))

    b_copy = remote(bsend, bpair, b_s, b_r, depth=k + 1 - 2 * core)

    def w_copy(c):
        return remote(wsend.at[rows_of(c)], wbuf.at[lane], w_s.at[c], w_r.at[lane], depth=2 * (half * span + c))

    def w_arrival(c):
        return remote(wsend.at[rows_of(c)], wbuf.at[c], w_s.at[c], w_r.at[c], depth=2 * (half * span + c))

    change = abuf[RELAX].astype(F32) - abuf[RELAX - 1].astype(F32)

    @pl.when(core == 1)
    def _():
        bsend[...] = times_t(change, own_d[...]).astype(BF16)
        b_copy.start()

    for s in range(RELAX, most):
        gather_step(s)

    @pl.when(core == 0)
    def _():
        b_copy.wait_recv()
        wsend[...] = times_t(change + bpair[...].astype(F32), own_d[...]).astype(BF16)
        for c in range(span):
            @pl.when(lane != c)
            def _(c=c):
                w_copy(c).start()

            @pl.when(lane == c)
            def _(c=c):
                wbuf[c] = wsend[rows_of(c), :]

        for c in range(span):
            @pl.when(lane != c)
            def _(c=c):
                w_arrival(c).wait_recv()

        @pl.when(half == 1)
        def _():
            crecv[1] = jnp.zeros((Q, D), BF16)

        @pl.when(half == 0)
        def _():
            c_back.wait_recv()

        y = crecv[1].astype(F32)
        for c in reversed(range(span)):
            zsend[c] = y.astype(BF16)
            give(zsend, zbuf, z_s, z_r, c)
            y = times_t(y, all_n[c]) + wbuf[c].astype(F32)

        @pl.when(half == 1)
        def _():
            csend[1] = y.astype(BF16)
            c_back.start()

        take(zsend, zbuf, z_s, z_r)
        corr[...] = (
            abuf[RELAX].astype(F32) + bpair[...].astype(F32) + times_t(zbuf[...].astype(F32), pair_d[...])
        )

    @pl.when(core == 1)
    def _():
        take(zsend, zbuf, z_s, z_r)
        corr[...] = abuf[RELAX].astype(F32) + zbuf[...].astype(F32)

    def w_sent():
        given(zsend, zbuf, z_s, z_r)
        for c in range(span):
            pl.when(lane != c)(w_copy(c).wait_send)
        pl.when(half == 1)(c_back.wait_send)

    on(core == 0, w_sent)
    on(core == 1, b_copy.wait_send)

    g = corr[...]
    rbuf[L + 1, z] = g.astype(BF16)
    ring_begin(L + 1)
    g = adjoint(g, 1)
    rbuf[L, z] = g.astype(BF16)
    ring_begin(L)

    gu[...] = jnp.zeros_like(gu)
    gd[...] = jnp.zeros_like(gd)

    def contract(layer, j):
        low = rbuf[L + layer, j]
        delta = (nt(low, wds[layer]) * slope_s[layer, j]).astype(BF16)
        gu[layer] += nn(norm_t[layer, j], delta)
        gd[layer] += nn(hid_t[layer, j], low)

    rows, part = D // ndp, D // 2
    other = (1 - x) * nz + z

    def x_copy(layer):
        return remote(
            gus.at[layer, pl.ds(pl.multiple_of((1 - x) * part, part), part)], gx.at[layer],
            x_s.at[layer], x_r.at[layer], dp=other,
        )

    def h_copy(layer):
        return remote(
            gds.at[layer, pl.ds(pl.multiple_of((1 - x) * F, F), F)], gdrecv.at[layer],
            h_s.at[layer], h_r.at[layer], dp=other,
        )

    def g_copy(layer, i):
        t = (z + i) % nz
        return remote(
            gsum.at[layer, pl.ds(pl.multiple_of(t * rows, rows), rows)], gurecv.at[layer, z],
            g_s.at[layer, i], g_r.at[layer, z], dp=x * nz + t,
        )

    def g_arrival(layer, i):
        t = (z + i) % nz
        return remote(
            gsum.at[layer, pl.ds(pl.multiple_of(t * rows, rows), rows)], gurecv.at[layer, t],
            g_s.at[layer, i], g_r.at[layer, t], dp=x * nz + t,
        )

    def send_halves(layer):
        gus[layer] = gu[layer].astype(BF16)
        x_copy(layer).start()
        gds[layer] = gd[layer].astype(BF16)
        h_copy(layer).start()
        pending.append(x_copy(layer).wait_send)
        pending.append(h_copy(layer).wait_send)

    contract(1, z)
    contract(0, z)
    for s in range(most):
        for layer in (1, 0):
            ring_step(L + layer, s)
        for layer in (1, 0):
            for way in range(2):
                if s < steps[layer][way]:
                    contract(layer, ring_slot(way, s))
            if s == most - 1:
                send_halves(layer)

    for layer in (1, 0):
        x_copy(layer).wait_recv()
        gsum[layer] = (gu[layer, pl.ds(pl.multiple_of(x * part, part), part), :] + gx[layer].astype(F32)).astype(BF16)
        each(1, nz, lambda i: g_copy(layer, i).start())
        gurecv[layer, z] = gsum[layer, pl.ds(pl.multiple_of(z * rows, rows), rows), :]
        pending.append(lambda layer=layer: each(1, nz, lambda i: g_copy(layer, i).wait_send()))

    for layer in (1, 0):
        h_copy(layer).wait_recv()
        gd_out[layer] = (
            gd[layer, pl.ds(pl.multiple_of(x * F, F), F), :] + gdrecv[layer].astype(F32)
        ).astype(BF16)
    for layer in (1, 0):
        each(1, nz, lambda i: g_arrival(layer, i).wait_recv())
        for j in range(nz):
            gu_out[layer, :, j * F:(j + 1) * F] = gurecv[layer, j, :, :F]
            gu_out[layer, :, FF // 2 + j * F:FF // 2 + (j + 1) * F] = gurecv[layer, j, :, F:]

    for wait in pending:
        wait()


def shards(nd, ndp, token_ids, embedding, w_up, w_down, cotangent):
    T, D = cotangent.shape
    L, _, FF = w_up.shape
    nz, nchip = ndp // 2, nd // 2
    span = max(nchip // 2, 1)
    R, Q, F = T // nchip, T // span, FF // ndp
    most = max(nz // 2, 1)
    V = pltpu.VMEM
    sem = pltpu.SemaphoreType.DMA
    scratch = [
        V((L, D, FF), BF16), V((L, FF, D), BF16), V(embedding.shape, BF16),
        V((nd, R, D // 2), BF16), V((nd, R, D // 2), BF16), V((nd, R, D // 2), BF16),
        V((D, D), BF16), V((D, D), BF16), V((span, D, D), BF16),
        V((RELAX + 1, T, D), BF16), V((RELAX, T, D), BF16), V((RELAX + 1, T, D), BF16), V((RELAX, T, D), BF16),
        V((T, D), BF16), V((T, D), BF16), V((T, D), BF16), V((span, Q, D), BF16), V((span, Q, D), BF16), V((T, D), BF16),
        V((T, D), BF16), V((T, D), BF16), V((T, D), BF16), V((span, Q, D), BF16), V((span, Q, D), BF16), V((T, D), BF16),
        V((T, D), F32), V((L, T, D), F32), V((L, T, 1), F32), V((L, T, FF), F32),
        V((2 * L, nz, T, D), BF16), V((L, D, 2 * F), BF16), V((L, 2 * F, D), BF16),
        V((L, nz, D, T), BF16), V((L, nz, 2 * F, T), BF16), V((L, nz, T, 2 * F), F32),
        V((L, D, 2 * F), F32), V((L, 2 * F, D), F32), V((L, D, 2 * F), BF16), V((L, 2 * F, D), BF16),
        V((L, nz, D // ndp, 2 * F), BF16), V((L, F, D), BF16), V((L, D // 2, 2 * F), BF16), V((L, D // 2, 2 * F), BF16),
        V((2, Q, D), BF16), V((2, Q, D), BF16),
        sem((3,)), sem((nd,)), sem((nd,)), sem((nd,)), sem((nd,)), sem, sem, sem((nchip,)), sem((nchip,)),
        sem((RELAX,)), sem((RELAX,)), sem((RELAX,)), sem((RELAX,)),
        sem, sem, sem((nchip,)), sem((nchip,)), sem((nchip, 2)), sem((nchip,)),
        sem, sem, sem((nchip,)), sem((nchip,)), sem((nchip, 2)), sem((nchip,)),
        sem((2 * L, 2, most)), sem((2 * L, 2, most)), sem((L, nz)), sem((L, nz)), sem((L,)), sem((L,)),
        sem((L,)), sem((L,)), sem((2,)), sem((2,)),
    ]
    vmem = pl.BlockSpec(memory_space=pltpu.VMEM)
    hbm = pl.BlockSpec(memory_space=pl.ANY)
    grad_up, grad_down = pl.pallas_call(
        functools.partial(kernel, nd, nz),
        out_shape=(
            jax.ShapeDtypeStruct((L, D // ndp, FF), BF16),
            jax.ShapeDtypeStruct((L, FF // ndp, D), BF16),
        ),
        in_specs=[vmem, hbm, hbm, hbm, vmem],
        out_specs=(vmem, vmem),
        scratch_shapes=scratch,
        compiler_params=pltpu.CompilerParams(
            collective_id=0, has_side_effects=True, vmem_limit_bytes=58 * 1024 * 1024
        ),
    )(token_ids[None, :], embedding, w_up, w_down, cotangent)
    return grad_up.astype(F32), grad_down.astype(F32)


def solution(mesh):
    in_specs = (
        P("dp"),
        P("depth", None),
        P("depth", None, None),
        P("depth", None, None),
        P("dp", None),
    )
    out_specs = (P("depth", "dp", None), P("depth", "dp", None))
    body = functools.partial(shards, mesh.shape["depth"], mesh.shape["dp"])
    return jax.shard_map(body, mesh=mesh, in_specs=in_specs, out_specs=out_specs, check_vma=False)
```

```python
import functools

import jax
import jax.numpy as jnp
from jax import lax
from jax.experimental import pallas as pl
from jax.experimental.pallas import tpu as pltpu
from jax.sharding import PartitionSpec as P

RELAX = 3
EPSILON = 1e-06
GAMMA = 0.05
F32, BF16 = jnp.float32, jnp.bfloat16
MESH = pl.DeviceIdType.MESH


def nn(a, b):
    return jnp.dot(a, b, preferred_element_type=F32)


def nt(a, b):
    return lax.dot_general(a, b, (((1,), (1,)), ((), ())), preferred_element_type=F32)


def sigmoid(p):
    return 0.5 * jnp.tanh(0.5 * p) + 0.5


def kernel(
    nd, nz,
    tok, emb_hbm, wu_hbm, wd_hbm, cot,
    gu_out, gd_out,
    wu, wd, emb,
    epick, erecv, estart,
    own_d, pair_d, all_n,
    cbuf, fsend, abuf, asend,
    tsend, tpair, usend, ubuf, ysend, ybuf,
    bsend, bpair, wsend, wbuf, zsend, zbuf,
    corr, unit, scales, slope,
    rbuf, wus, wds, norm_t, hid_t, slope_s,
    gu, gd, gus, gds, gurecv, gdrecv, csend, crecv,
    load_sem, e_s, e_r, e2_s, e2_r, d_s, d_r, n_s, n_r,
    f_s, f_r, a_s, a_r, t_s, t_r, u_s, u_r, y_s, y_r,
    b_s, b_r, w_s, w_r, z_s, z_r, ring_s, ring_r, g_s, g_r, h_s, h_r, c_s, c_r,
):
    T, D = cot.shape
    L, _, FF = wu.shape
    ndp, nchip = 2 * nz, nd // 2
    k, p = lax.axis_index("depth"), lax.axis_index("dp")
    core, chip = k % 2, k // 2
    span = max(nchip // 2, 1)
    half, lane = chip // span, chip % span
    Q = T // span
    x, z = p // nz, p % nz
    F = FF // ndp
    vocab = emb.shape[0]
    wide = min(512, FF)

    def remote(src, dst, ssem, rsem, depth=k, dp=p):
        return pltpu.make_async_remote_copy(
            src_ref=src, dst_ref=dst, send_sem=ssem, recv_sem=rsem,
            device_id={"depth": depth, "dp": dp}, device_id_type=MESH,
        )

    load_up = pltpu.make_async_copy(wu_hbm, wu, load_sem.at[0])
    load_down = pltpu.make_async_copy(wd_hbm, wd, load_sem.at[1])
    load_rows = pltpu.make_async_copy(emb_hbm, emb, load_sem.at[2])
    load_rows.start()
    load_up.start()
    load_down.start()

    barrier = pltpu.get_barrier_semaphore()
    pending = []

    def greet_depth(i, c):
        pl.semaphore_signal(barrier, inc=1, device_id={"depth": (k + i) % nd, "dp": p}, device_id_type=MESH)
        return c

    def greet_dp(i, c):
        pl.semaphore_signal(barrier, inc=1, device_id={"depth": k, "dp": (p + i) % ndp}, device_id_type=MESH)
        return c

    lax.fori_loop(1, nd, greet_depth, 0)
    lax.fori_loop(1, ndp, greet_dp, 0)

    R, H = T // nchip, D // 2
    load_rows.wait()
    local = jnp.broadcast_to(tok[...] - k * vocab, (T, T)).T[:, :1]
    onehot = (local == lax.broadcasted_iota(jnp.int32, (T, vocab), 1)).astype(BF16)
    picked = nn(onehot, emb[...]).astype(BF16)
    for c in range(nd):
        epick[c] = picked[(c // 2) * R:(c // 2 + 1) * R, (c % 2) * H:(c % 2 + 1) * H]
    pl.semaphore_wait(barrier, nd + ndp - 2)

    def pick_copy(i):
        t = (k + i) % nd
        return remote(epick.at[t], erecv.at[k], e_s.at[i], e_r.at[k], depth=t)

    def pick_arrival(i):
        t = (k + i) % nd
        return remote(epick.at[t], erecv.at[t], e_s.at[i], e_r.at[t], depth=t)

    def start_copy(i):
        t = (k + i) % nd
        return remote(estart.at[k], estart.at[k], e2_s.at[i], e2_r.at[k], depth=t)

    def start_arrival(i):
        t = (k + i) % nd
        return remote(estart.at[t], estart.at[t], e2_s.at[i], e2_r.at[t], depth=t)

    def each(low, high, f):
        def body(i, c):
            f(i)
            return c
        lax.fori_loop(low, high, body, 0)

    each(1, nd, lambda i: pick_copy(i).start())
    pending.append(lambda: each(1, nd, lambda i: pick_copy(i).wait_send()))
    erecv[k] = epick[k]

    load_up.wait()
    load_down.wait()

    def coarse_rows(i):
        rows = pl.ds(pl.multiple_of(i * 128, 128), 128)
        total = nn(wu[0, rows, :], wd[0])
        total = total + nn(wu[1, rows, :], wd[1])
        own_d[rows, :] = (GAMMA * total).astype(BF16)

    each(0, D // 128, coarse_rows)
    d_copy = remote(own_d, pair_d, d_s, d_r, depth=k + 1 - 2 * core)
    d_copy.start()
    pending.append(d_copy.wait_send)

    each(1, nd, lambda i: pick_arrival(i).wait_recv())
    total = erecv[0].astype(F32)
    for c in range(1, nd):
        total = total + erecv[c].astype(F32)
    estart[k] = total.astype(BF16)
    each(1, nd, lambda i: start_copy(i).start())
    pending.append(lambda: each(1, nd, lambda i: start_copy(i).wait_send()))

    d_copy.wait_recv()

    def n_copy(i):
        t = (lane + i) % span
        return remote(all_n.at[lane], all_n.at[lane], n_s.at[i], n_r.at[lane], depth=2 * (half * span + t))

    def n_arrival(i):
        t = (lane + i) % span
        return remote(all_n.at[t], all_n.at[t], n_s.at[i], n_r.at[t], depth=2 * (half * span + t))

    def combine(first, second):
        product = nn(first[...], second[...])
        all_n[lane] = (product + first[...].astype(F32) + second[...].astype(F32)).astype(BF16)

    @pl.when(core == 1)
    def _():
        combine(pair_d, own_d)

    @pl.when(core == 0)
    def _():
        combine(own_d, pair_d)
        each(1, span, lambda i: n_copy(i).start())

    def on(condition, f):
        pending.append(lambda: pl.when(condition)(f))

    on(core == 0, lambda: each(1, span, lambda i: n_copy(i).wait_send()))

    for piece in range(2):
        at = pl.multiple_of(piece * (FF // 2) + z * F, 128)
        for layer in range(L):
            wus[layer, :, piece * F:(piece + 1) * F] = wu[layer, :, pl.ds(at, F)]
            wds[layer, piece * F:(piece + 1) * F, :] = wd[layer, pl.ds(at, F), :]

    each(1, nd, lambda i: start_arrival(i).wait_recv())
    for c in range(nd):
        cbuf[0, (c // 2) * R:(c // 2 + 1) * R, (c % 2) * H:(c % 2 + 1) * H] = estart[c]

    def forward(v, layer, save):
        scale = lax.rsqrt(jnp.mean(v * v, axis=-1, keepdims=True) + EPSILON)
        n = v * scale
        normed = n.astype(BF16)
        if save:
            unit[layer] = n
            scales[layer] = scale
            rbuf[layer, z] = normed
        total = None
        for at in range(0, FF, wide):
            pre = nn(normed, wu[layer, :, at:at + wide])
            s = sigmoid(pre)
            if save:
                slope[layer, :, at:at + wide] = s * (1.0 + pre * (1.0 - s))
            part = nn((pre * s).astype(BF16), wd[layer, at:at + wide, :])
            total = part if total is None else total + part
        return v + total

    def adjoint(g, layer):
        low = g.astype(BF16)
        q = None
        for at in range(0, FF, wide):
            toward = nt(low, wd[layer, at:at + wide, :])
            delta = (toward * slope[layer, :, at:at + wide]).astype(BF16)
            part = nt(delta, wu[layer, :, at:at + wide])
            q = part if q is None else q + part
        n = unit[layer]
        inner = jnp.mean(q * n, axis=-1, keepdims=True)
        return g + scales[layer] * (q - n * inner)

    def f_copy(s):
        return remote(fsend.at[s], cbuf.at[s + 1], f_s.at[s], f_r.at[s], depth=(k + 1) % nd)

    def forward_sweep(s):
        v = cbuf[s].astype(F32)
        for layer in range(L):
            v = forward(v, layer, False)
        fsend[s] = v.astype(BF16)

        @pl.when(k < nd - 1)
        def _():
            f_copy(s).start()

        @pl.when(k > 0)
        def _():
            f_copy(s).wait_recv()

        @pl.when(k == 0)
        def _():
            cbuf[s + 1] = cbuf[0]

    each(0, RELAX, forward_sweep)
    on(k < nd - 1, lambda: each(0, RELAX, lambda s: f_copy(s).wait_send()))

    def times(v, d):
        return v + nn(v.astype(BF16), d)

    def times_t(v, d):
        return v + nt(v.astype(BF16), d)

    t_copy = remote(tsend, tpair, t_s, t_r, depth=k + 1 - 2 * core)

    def rows_of(c):
        return pl.ds(c * Q, Q)

    def u_copy(c):
        return remote(usend.at[rows_of(c)], ubuf.at[core, lane], u_s.at[c], u_r.at[core, lane], depth=2 * (half * span + c))

    def u_arrival(j, c):
        return remote(usend.at[rows_of(c)], ubuf.at[j, c], u_s.at[c], u_r.at[j, c], depth=2 * (half * span + c))

    def spread(src, dst, copy):
        for c in range(span):
            @pl.when((core == 1) | (lane != c))
            def _(c=c):
                copy(c).start()

            @pl.when((core == 0) & (lane == c))
            def _(c=c):
                dst[0, c] = src[rows_of(c), :]

    def collect(arrival):
        for c in range(span):
            arrival(1, c).wait_recv()

            @pl.when(lane != c)
            def _(c=c):
                arrival(0, c).wait_recv()

    def spread_sent(copy):
        for c in range(span):
            pl.when((core == 1) | (lane != c))(copy(c).wait_send)

    def both_of(buf, c):
        return buf[0, c].astype(F32) + buf[1, c].astype(F32)

    mine = pl.ds(pl.multiple_of(lane * Q, Q), Q)

    def y_copy(src, dst, ss, rs, c, to):
        return remote(src.at[c], dst.at[mine], ss.at[c, to], rs.at[lane], depth=2 * (half * span + c) + to)

    def y_arrival(src, dst, ss, rs, c):
        return remote(src.at[c], dst.at[rows_of(c)], ss.at[c, 0], rs.at[c], depth=2 * (half * span + c))

    def give(src, dst, ss, rs, c):
        y_copy(src, dst, ss, rs, c, 1).start()

        @pl.when(lane != c)
        def _():
            y_copy(src, dst, ss, rs, c, 0).start()

        @pl.when(lane == c)
        def _():
            dst[mine, :] = src[c]

    def take(src, dst, ss, rs):
        for c in range(span):
            @pl.when((core == 1) | (lane != c))
            def _(c=c):
                y_arrival(src, dst, ss, rs, c).wait_recv()

    across = (k + nchip) % nd
    c_copy = remote(csend.at[0], crecv.at[0], c_s.at[0], c_r.at[0], depth=across)
    c_back = remote(csend.at[1], crecv.at[1], c_s.at[1], c_r.at[1], depth=across)

    change = cbuf[RELAX].astype(F32) - cbuf[RELAX - 1].astype(F32)

    @pl.when(core == 0)
    def _():
        usend[...] = times(change, all_n[lane]).astype(BF16)

    @pl.when(core == 1)
    def _():
        usend[...] = times(change, own_d[...]).astype(BF16)

    spread(usend, ubuf, u_copy)
    pending.append(lambda: spread_sent(u_copy))

    @pl.when(core == 0)
    def _():
        tsend[...] = times(change, own_d[...]).astype(BF16)
        t_copy.start()
        each(1, span, lambda i: n_arrival(i).wait_recv())
        collect(u_arrival)

        @pl.when(half == 0)
        def _():
            crecv[0] = jnp.zeros((Q, D), BF16)

        @pl.when(half == 1)
        def _():
            c_copy.wait_recv()

        y = crecv[0].astype(F32)
        for c in range(span):
            ysend[c] = y.astype(BF16)
            give(ysend, ybuf, y_s, y_r, c)
            y = times(y, all_n[c]) + both_of(ubuf, c)

        @pl.when(half == 0)
        def _():
            csend[0] = y.astype(BF16)
            c_copy.start()

        take(ysend, ybuf, y_s, y_r)
        corr[...] = cbuf[RELAX].astype(F32) + ybuf[...].astype(F32)

    @pl.when(core == 1)
    def _():
        t_copy.wait_recv()
        take(ysend, ybuf, y_s, y_r)
        corr[...] = (
            cbuf[RELAX].astype(F32) + tpair[...].astype(F32) + times(ybuf[...].astype(F32), pair_d[...])
        )

    def given(src, dst, ss, rs):
        for c in range(span):
            y_copy(src, dst, ss, rs, c, 1).wait_send()
            pl.when(lane != c)(y_copy(src, dst, ss, rs, c, 0).wait_send)

    def scan_sent():
        t_copy.wait_send()
        given(ysend, ybuf, y_s, y_r)
        pl.when(half == 0)(c_copy.wait_send)

    on(core == 0, scan_sent)

    steps = ((nz // 2, nz - 1 - nz // 2), (nz - 1 - nz // 2, nz // 2))
    most = nz // 2

    def ring_copy(r, way, s):
        slot = (z - s + nz) % nz if way == 0 else (z + s) % nz
        to = (z + 1) % nz if way == 0 else (z + nz - 1) % nz
        return remote(rbuf.at[r, slot], rbuf.at[r, slot], ring_s.at[r, way, s], ring_r.at[r, way, s], dp=x * nz + to)

    def ring_slot(way, s):
        return (z - s - 1 + nz) % nz if way == 0 else (z + s + 1) % nz

    def ring_arrival(r, way, s):
        slot = ring_slot(way, s)
        to = (z + 1) % nz if way == 0 else (z + nz - 1) % nz
        return remote(rbuf.at[r, slot], rbuf.at[r, slot], ring_s.at[r, way, s], ring_r.at[r, way, s], dp=x * nz + to)

    def ring_begin(r):
        pending.append(lambda: ring_end(r))
        for way in range(2):
            if steps[r % 2][way] > 0:
                ring_copy(r, way, 0).start()

    def ring_step(r, s):
        for way in range(2):
            if s < steps[r % 2][way]:
                ring_arrival(r, way, s).wait_recv()
                if s + 1 < steps[r % 2][way]:
                    ring_copy(r, way, s + 1).start()

    def ring_end(r):
        for way in range(2):
            for s in range(steps[r % 2][way]):
                ring_copy(r, way, s).wait_send()

    def prepare(layer, j):
        normed = rbuf[layer, j]
        norm_t[layer, j] = normed.T
        pre = nn(normed, wus[layer])
        s = sigmoid(pre)
        hid_t[layer, j] = (pre * s).astype(BF16).T
        slope_s[layer, j] = s * (1.0 + pre * (1.0 - s))

    def gather_step(s):
        for layer in range(L):
            ring_step(layer, s)

    v = corr[...]
    for layer in range(L):
        v = forward(v, layer, True)
        ring_begin(layer)

    def a_copy(s):
        return remote(asend.at[s], abuf.at[s + 1], a_s.at[s], a_r.at[s], depth=(k + nd - 1) % nd)

    abuf[0] = cot[...]

    for s in range(RELAX):
        g = abuf[s].astype(F32)
        for layer in reversed(range(L)):
            g = adjoint(g, layer)
        asend[s] = g.astype(BF16)

        @pl.when(k > 0)
        def _():
            a_copy(s).start()

        if s < most:
            gather_step(s)

        @pl.when(k < nd - 1)
        def _():
            a_copy(s).wait_recv()

        @pl.when(k == nd - 1)
        def _():
            abuf[s + 1] = abuf[0]

    on(k > 0, lambda: each(0, RELAX, lambda s: a_copy(s).wait_send()))

    b_copy = remote(bsend, bpair, b_s, b_r, depth=k + 1 - 2 * core)

    def w_copy(c):
        return remote(wsend.at[rows_of(c)], wbuf.at[core, lane], w_s.at[c], w_r.at[core, lane], depth=2 * (half * span + c))

    def w_arrival(j, c):
        return remote(wsend.at[rows_of(c)], wbuf.at[j, c], w_s.at[c], w_r.at[j, c], depth=2 * (half * span + c))

    change = abuf[RELAX].astype(F32) - abuf[RELAX - 1].astype(F32)

    @pl.when(core == 1)
    def _():
        wsend[...] = times_t(change, all_n[lane]).astype(BF16)

    @pl.when(core == 0)
    def _():
        wsend[...] = times_t(change, own_d[...]).astype(BF16)

    spread(wsend, wbuf, w_copy)
    pending.append(lambda: spread_sent(w_copy))

    @pl.when(core == 1)
    def _():
        bsend[...] = times_t(change, own_d[...]).astype(BF16)
        b_copy.start()

    for s in range(RELAX, most):
        gather_step(s)

    @pl.when(core == 0)
    def _():
        collect(w_arrival)

        @pl.when(half == 1)
        def _():
            crecv[1] = jnp.zeros((Q, D), BF16)

        @pl.when(half == 0)
        def _():
            c_back.wait_recv()

        y = crecv[1].astype(F32)
        for c in reversed(range(span)):
            zsend[c] = y.astype(BF16)
            give(zsend, zbuf, z_s, z_r, c)
            y = times_t(y, all_n[c]) + both_of(wbuf, c)

        @pl.when(half == 1)
        def _():
            csend[1] = y.astype(BF16)
            c_back.start()

    def prepare_slot(j):
        for layer in range(L):
            prepare(layer, j)

    each(0, nz, prepare_slot)

    @pl.when(core == 0)
    def _():
        b_copy.wait_recv()
        take(zsend, zbuf, z_s, z_r)
        corr[...] = (
            abuf[RELAX].astype(F32) + bpair[...].astype(F32) + times_t(zbuf[...].astype(F32), pair_d[...])
        )

    @pl.when(core == 1)
    def _():
        take(zsend, zbuf, z_s, z_r)
        corr[...] = abuf[RELAX].astype(F32) + zbuf[...].astype(F32)

    def w_sent():
        given(zsend, zbuf, z_s, z_r)
        pl.when(half == 1)(c_back.wait_send)

    on(core == 0, w_sent)
    on(core == 1, b_copy.wait_send)

    g = corr[...]
    rbuf[L + 1, z] = g.astype(BF16)
    ring_begin(L + 1)
    g = adjoint(g, 1)
    rbuf[L, z] = g.astype(BF16)
    ring_begin(L)

    gu[...] = jnp.zeros_like(gu)
    gd[...] = jnp.zeros_like(gd)

    def contract(layer, j):
        low = rbuf[L + layer, j]
        delta = (nt(low, wds[layer]) * slope_s[layer, j]).astype(BF16)
        gu[layer] += nn(norm_t[layer, j], delta)
        gd[layer] += nn(hid_t[layer, j], low)

    rows = D // ndp

    def h_copy(layer):
        return remote(
            gds.at[layer, pl.ds(pl.multiple_of((1 - x) * F, F), F)], gdrecv.at[layer],
            h_s.at[layer], h_r.at[layer], dp=(1 - x) * nz + z,
        )

    def g_copy(layer, i):
        t = (p + i) % ndp
        return remote(
            gus.at[layer, pl.ds(pl.multiple_of(t * rows, rows), rows)], gurecv.at[layer, p],
            g_s.at[layer, i], g_r.at[layer, p], dp=t,
        )

    def g_arrival(layer, i):
        t = (p + i) % ndp
        return remote(
            gus.at[layer, pl.ds(pl.multiple_of(t * rows, rows), rows)], gurecv.at[layer, t],
            g_s.at[layer, i], g_r.at[layer, t], dp=t,
        )

    def send_sums(layer):
        gds[layer] = gd[layer].astype(BF16)
        h_copy(layer).start()
        gus[layer] = gu[layer].astype(BF16)
        each(1, ndp, lambda i: g_copy(layer, i).start())
        gurecv[layer, p] = gus[layer, pl.ds(pl.multiple_of(p * rows, rows), rows), :]
        pending.append(h_copy(layer).wait_send)
        pending.append(lambda: each(1, ndp, lambda i: g_copy(layer, i).wait_send()))

    contract(1, z)
    contract(0, z)
    for s in range(most):
        for layer in (1, 0):
            ring_step(L + layer, s)
        for layer in (1, 0):
            for way in range(2):
                if s < steps[layer][way]:
                    contract(layer, ring_slot(way, s))
            if s == most - 1:
                send_sums(layer)

    for layer in (1, 0):
        h_copy(layer).wait_recv()
        gd_out[layer] = (
            gd[layer, pl.ds(pl.multiple_of(x * F, F), F), :] + gdrecv[layer].astype(F32)
        ).astype(BF16)
        each(1, ndp, lambda i: g_arrival(layer, i).wait_recv())
        for j in range(nz):
            both = (gurecv[layer, j].astype(F32) + gurecv[layer, nz + j].astype(F32)).astype(BF16)
            gu_out[layer, :, j * F:(j + 1) * F] = both[:, :F]
            gu_out[layer, :, FF // 2 + j * F:FF // 2 + (j + 1) * F] = both[:, F:]

    for wait in pending:
        wait()


def shards(nd, ndp, token_ids, embedding, w_up, w_down, cotangent):
    T, D = cotangent.shape
    L, _, FF = w_up.shape
    nz, nchip = ndp // 2, nd // 2
    span = max(nchip // 2, 1)
    R, Q, F = T // nchip, T // span, FF // ndp
    most = max(nz // 2, 1)
    V = pltpu.VMEM
    sem = pltpu.SemaphoreType.DMA
    scratch = [
        V((L, D, FF), BF16), V((L, FF, D), BF16), V(embedding.shape, BF16),
        V((nd, R, D // 2), BF16), V((nd, R, D // 2), BF16), V((nd, R, D // 2), BF16),
        V((D, D), BF16), V((D, D), BF16), V((span, D, D), BF16),
        V((RELAX + 1, T, D), BF16), V((RELAX, T, D), BF16), V((RELAX + 1, T, D), BF16), V((RELAX, T, D), BF16),
        V((T, D), BF16), V((T, D), BF16), V((T, D), BF16), V((2, span, Q, D), BF16), V((span, Q, D), BF16), V((T, D), BF16),
        V((T, D), BF16), V((T, D), BF16), V((T, D), BF16), V((2, span, Q, D), BF16), V((span, Q, D), BF16), V((T, D), BF16),
        V((T, D), F32), V((L, T, D), F32), V((L, T, 1), F32), V((L, T, FF), F32),
        V((2 * L, nz, T, D), BF16), V((L, D, 2 * F), BF16), V((L, 2 * F, D), BF16),
        V((L, nz, D, T), BF16), V((L, nz, 2 * F, T), BF16), V((L, nz, T, 2 * F), F32),
        V((L, D, 2 * F), F32), V((L, 2 * F, D), F32), V((L, D, 2 * F), BF16), V((L, 2 * F, D), BF16),
        V((L, ndp, D // ndp, 2 * F), BF16), V((L, F, D), BF16),
        V((2, Q, D), BF16), V((2, Q, D), BF16),
        sem((3,)), sem((nd,)), sem((nd,)), sem((nd,)), sem((nd,)), sem, sem, sem((nchip,)), sem((nchip,)),
        sem((RELAX,)), sem((RELAX,)), sem((RELAX,)), sem((RELAX,)),
        sem, sem, sem((nchip,)), sem((2, nchip)), sem((nchip, 2)), sem((nchip,)),
        sem, sem, sem((nchip,)), sem((2, nchip)), sem((nchip, 2)), sem((nchip,)),
        sem((2 * L, 2, most)), sem((2 * L, 2, most)), sem((L, ndp)), sem((L, ndp)), sem((L,)), sem((L,)), sem((2,)), sem((2,)),
    ]
    vmem = pl.BlockSpec(memory_space=pltpu.VMEM)
    hbm = pl.BlockSpec(memory_space=pl.ANY)
    grad_up, grad_down = pl.pallas_call(
        functools.partial(kernel, nd, nz),
        out_shape=(
            jax.ShapeDtypeStruct((L, D // ndp, FF), BF16),
            jax.ShapeDtypeStruct((L, FF // ndp, D), BF16),
        ),
        in_specs=[vmem, hbm, hbm, hbm, vmem],
        out_specs=(vmem, vmem),
        scratch_shapes=scratch,
        compiler_params=pltpu.CompilerParams(
            collective_id=0, has_side_effects=True, vmem_limit_bytes=58 * 1024 * 1024
        ),
    )(token_ids[None, :], embedding, w_up, w_down, cotangent)
    return grad_up.astype(F32), grad_down.astype(F32)


def solution(mesh):
    in_specs = (
        P("dp"),
        P("depth", None),
        P("depth", None, None),
        P("depth", None, None),
        P("dp", None),
    )
    out_specs = (P("depth", "dp", None), P("depth", "dp", None))
    body = functools.partial(shards, mesh.shape["depth"], mesh.shape["dp"])
    return jax.shard_map(body, mesh=mesh, in_specs=in_specs, out_specs=out_specs, check_vma=False)
```

```python
import functools

import jax
import jax.numpy as jnp
from jax import lax
from jax.experimental import pallas as pl
from jax.experimental.pallas import tpu as pltpu
from jax.sharding import PartitionSpec as P

RELAX = 3
EPSILON = 1e-06
GAMMA = 0.05
F32, BF16 = jnp.float32, jnp.bfloat16
MESH = pl.DeviceIdType.MESH


def nn(a, b):
    return jnp.dot(a, b, preferred_element_type=F32)


def nt(a, b):
    return lax.dot_general(a, b, (((1,), (1,)), ((), ())), preferred_element_type=F32)


def sigmoid(p):
    return 0.5 * jnp.tanh(0.5 * p) + 0.5


def kernel(
    nd, nz,
    tok, emb_hbm, wu_hbm, wd_hbm, cot,
    gu_out, gd_out,
    wu, wd, emb,
    epick, erecv, estart,
    own_d, pair_d, all_n,
    cbuf, fsend, abuf, asend,
    tsend, tpair, usend, ubuf, ysend, ybuf,
    bsend, bpair, wsend, wbuf, zsend, zbuf,
    corr, unit, scales, slope,
    rbuf, wus, wds, norm_t, hid_t, slope_s,
    gu, gd, gus, gds, gurecv, gdrecv, csend, crecv,
    load_sem, e_s, e_r, e2_s, e2_r, d_s, d_r, n_s, n_r,
    f_s, f_r, a_s, a_r, t_s, t_r, u_s, u_r, y_s, y_r,
    b_s, b_r, w_s, w_r, z_s, z_r, ring_s, ring_r, g_s, g_r, h_s, h_r, c_s, c_r,
):
    T, D = cot.shape
    L, _, FF = wu.shape
    ndp, nchip = 2 * nz, nd // 2
    k, p = lax.axis_index("depth"), lax.axis_index("dp")
    core, chip = k % 2, k // 2
    span = max(nchip // 2, 1)
    half, lane = chip // span, chip % span
    Q = T // span
    x, z = p // nz, p % nz
    F = FF // ndp
    vocab = emb.shape[0]
    wide = min(512, FF)

    def remote(src, dst, ssem, rsem, depth=k, dp=p):
        return pltpu.make_async_remote_copy(
            src_ref=src, dst_ref=dst, send_sem=ssem, recv_sem=rsem,
            device_id={"depth": depth, "dp": dp}, device_id_type=MESH,
        )

    load_up = pltpu.make_async_copy(wu_hbm, wu, load_sem.at[0])
    load_down = pltpu.make_async_copy(wd_hbm, wd, load_sem.at[1])
    load_rows = pltpu.make_async_copy(emb_hbm, emb, load_sem.at[2])
    load_rows.start()
    load_up.start()
    load_down.start()

    barrier = pltpu.get_barrier_semaphore()
    pending = []

    def greet_depth(i, c):
        pl.semaphore_signal(barrier, inc=1, device_id={"depth": (k + i) % nd, "dp": p}, device_id_type=MESH)
        return c

    def greet_dp(i, c):
        pl.semaphore_signal(barrier, inc=1, device_id={"depth": k, "dp": (p + i) % ndp}, device_id_type=MESH)
        return c

    lax.fori_loop(1, nd, greet_depth, 0)
    lax.fori_loop(1, ndp, greet_dp, 0)

    R, H = T // nchip, D // 2
    load_rows.wait()
    local = jnp.broadcast_to(tok[...] - k * vocab, (T, T)).T[:, :1]
    onehot = (local == lax.broadcasted_iota(jnp.int32, (T, vocab), 1)).astype(BF16)
    picked = nn(onehot, emb[...]).astype(BF16)
    for c in range(nd):
        epick[c] = picked[(c // 2) * R:(c // 2 + 1) * R, (c % 2) * H:(c % 2 + 1) * H]
    pl.semaphore_wait(barrier, nd + ndp - 2)

    def pick_copy(i):
        t = (k + i) % nd
        return remote(epick.at[t], erecv.at[k], e_s.at[i], e_r.at[k], depth=t)

    def pick_arrival(i):
        t = (k + i) % nd
        return remote(epick.at[t], erecv.at[t], e_s.at[i], e_r.at[t], depth=t)

    def start_copy(i):
        t = (k + i) % nd
        return remote(estart.at[k], estart.at[k], e2_s.at[i], e2_r.at[k], depth=t)

    def start_arrival(i):
        t = (k + i) % nd
        return remote(estart.at[t], estart.at[t], e2_s.at[i], e2_r.at[t], depth=t)

    def each(low, high, f):
        def body(i, c):
            f(i)
            return c
        lax.fori_loop(low, high, body, 0)

    each(1, nd, lambda i: pick_copy(i).start())
    pending.append(lambda: each(1, nd, lambda i: pick_copy(i).wait_send()))
    erecv[k] = epick[k]

    load_up.wait()
    load_down.wait()

    def coarse_rows(i):
        rows = pl.ds(pl.multiple_of(i * 128, 128), 128)
        total = nn(wu[0, rows, :], wd[0])
        total = total + nn(wu[1, rows, :], wd[1])
        own_d[rows, :] = (GAMMA * total).astype(BF16)

    each(0, D // 256, coarse_rows)
    d_copy = remote(own_d, pair_d, d_s, d_r, depth=k + 1 - 2 * core)

    each(1, nd, lambda i: pick_arrival(i).wait_recv())
    total = erecv[0].astype(F32)
    for c in range(1, nd):
        total = total + erecv[c].astype(F32)
    estart[k] = total.astype(BF16)
    each(1, nd, lambda i: start_copy(i).start())
    pending.append(lambda: each(1, nd, lambda i: start_copy(i).wait_send()))

    each(D // 256, D // 128, coarse_rows)
    d_copy.start()
    pending.append(d_copy.wait_send)

    def n_copy(i):
        t = (lane + i) % span
        return remote(all_n.at[lane], all_n.at[lane], n_s.at[i], n_r.at[lane], depth=2 * (half * span + t))

    def n_arrival(i):
        t = (lane + i) % span
        return remote(all_n.at[t], all_n.at[t], n_s.at[i], n_r.at[t], depth=2 * (half * span + t))

    def combine(first, second):
        product = nn(first[...], second[...])
        all_n[lane] = (product + first[...].astype(F32) + second[...].astype(F32)).astype(BF16)

    def share():
        d_copy.wait_recv()

        @pl.when(core == 1)
        def _():
            combine(pair_d, own_d)

        @pl.when(core == 0)
        def _():
            combine(own_d, pair_d)
            each(1, span, lambda i: n_copy(i).start())

        for piece in range(2):
            at = pl.multiple_of(piece * (FF // 2) + z * F, 128)
            for layer in range(L):
                wus[layer, :, piece * F:(piece + 1) * F] = wu[layer, :, pl.ds(at, F)]
                wds[layer, piece * F:(piece + 1) * F, :] = wd[layer, pl.ds(at, F), :]

    def on(condition, f):
        pending.append(lambda: pl.when(condition)(f))

    on(core == 0, lambda: each(1, span, lambda i: n_copy(i).wait_send()))

    each(1, nd, lambda i: start_arrival(i).wait_recv())
    for c in range(nd):
        cbuf[0, (c // 2) * R:(c // 2 + 1) * R, (c % 2) * H:(c % 2 + 1) * H] = estart[c]

    def forward(v, layer, save):
        scale = lax.rsqrt(jnp.mean(v * v, axis=-1, keepdims=True) + EPSILON)
        n = v * scale
        normed = n.astype(BF16)
        if save:
            unit[layer] = n
            scales[layer] = scale
            rbuf[layer, z] = normed
        total = None
        for at in range(0, FF, wide):
            pre = nn(normed, wu[layer, :, at:at + wide])
            s = sigmoid(pre)
            if save:
                slope[layer, :, at:at + wide] = s * (1.0 + pre * (1.0 - s))
            part = nn((pre * s).astype(BF16), wd[layer, at:at + wide, :])
            total = part if total is None else total + part
        return v + total

    def adjoint(g, layer):
        low = g.astype(BF16)
        q = None
        for at in range(0, FF, wide):
            toward = nt(low, wd[layer, at:at + wide, :])
            delta = (toward * slope[layer, :, at:at + wide]).astype(BF16)
            part = nt(delta, wu[layer, :, at:at + wide])
            q = part if q is None else q + part
        n = unit[layer]
        inner = jnp.mean(q * n, axis=-1, keepdims=True)
        return g + scales[layer] * (q - n * inner)

    def f_copy(s):
        return remote(fsend.at[s], cbuf.at[s + 1], f_s.at[s], f_r.at[s], depth=(k + 1) % nd)

    def forward_sweep(s):
        v = cbuf[s].astype(F32)
        for layer in range(L):
            v = forward(v, layer, False)
        fsend[s] = v.astype(BF16)

        @pl.when(k < nd - 1)
        def _():
            f_copy(s).start()

        pl.when(s == 0)(share)

        @pl.when(k > 0)
        def _():
            f_copy(s).wait_recv()

        @pl.when(k == 0)
        def _():
            cbuf[s + 1] = cbuf[0]

    each(0, RELAX, forward_sweep)
    on(k < nd - 1, lambda: each(0, RELAX, lambda s: f_copy(s).wait_send()))

    def times(v, d):
        return v + nn(v.astype(BF16), d)

    def times_t(v, d):
        return v + nt(v.astype(BF16), d)

    t_copy = remote(tsend, tpair, t_s, t_r, depth=k + 1 - 2 * core)

    def rows_of(c):
        return pl.ds(c * Q, Q)

    def u_copy(c):
        return remote(usend.at[rows_of(c)], ubuf.at[core, lane], u_s.at[c], u_r.at[core, lane], depth=2 * (half * span + c))

    def u_arrival(j, c):
        return remote(usend.at[rows_of(c)], ubuf.at[j, c], u_s.at[c], u_r.at[j, c], depth=2 * (half * span + c))

    def spread(src, dst, copy):
        for c in range(span):
            @pl.when((core == 1) | (lane != c))
            def _(c=c):
                copy(c).start()

            @pl.when((core == 0) & (lane == c))
            def _(c=c):
                dst[0, c] = src[rows_of(c), :]

    def collect(arrival):
        for c in range(span):
            arrival(1, c).wait_recv()

            @pl.when(lane != c)
            def _(c=c):
                arrival(0, c).wait_recv()

    def spread_sent(copy):
        for c in range(span):
            pl.when((core == 1) | (lane != c))(copy(c).wait_send)

    def both_of(buf, c):
        return buf[0, c].astype(F32) + buf[1, c].astype(F32)

    mine = pl.ds(pl.multiple_of(lane * Q, Q), Q)

    def y_copy(src, dst, ss, rs, c, to):
        return remote(src.at[c], dst.at[mine], ss.at[c, to], rs.at[lane], depth=2 * (half * span + c) + to)

    def y_arrival(src, dst, ss, rs, c):
        return remote(src.at[c], dst.at[rows_of(c)], ss.at[c, 0], rs.at[c], depth=2 * (half * span + c))

    def give(src, dst, ss, rs, c):
        y_copy(src, dst, ss, rs, c, 1).start()

        @pl.when(lane != c)
        def _():
            y_copy(src, dst, ss, rs, c, 0).start()

        @pl.when(lane == c)
        def _():
            dst[mine, :] = src[c]

    def take(src, dst, ss, rs):
        for c in range(span):
            @pl.when((core == 1) | (lane != c))
            def _(c=c):
                y_arrival(src, dst, ss, rs, c).wait_recv()

    across = (k + nchip) % nd
    c_copy = remote(csend.at[0], crecv.at[0], c_s.at[0], c_r.at[0], depth=across)
    c_back = remote(csend.at[1], crecv.at[1], c_s.at[1], c_r.at[1], depth=across)

    change = cbuf[RELAX].astype(F32) - cbuf[RELAX - 1].astype(F32)

    @pl.when(core == 0)
    def _():
        usend[...] = times(change, all_n[lane]).astype(BF16)

    @pl.when(core == 1)
    def _():
        usend[...] = times(change, own_d[...]).astype(BF16)

    spread(usend, ubuf, u_copy)
    pending.append(lambda: spread_sent(u_copy))

    @pl.when(core == 0)
    def _():
        tsend[...] = times(change, own_d[...]).astype(BF16)
        t_copy.start()
        each(1, span, lambda i: n_arrival(i).wait_recv())
        collect(u_arrival)

        @pl.when(half == 0)
        def _():
            crecv[0] = jnp.zeros((Q, D), BF16)

        @pl.when(half == 1)
        def _():
            c_copy.wait_recv()

        y = crecv[0].astype(F32)
        for c in range(span):
            ysend[c] = y.astype(BF16)
            give(ysend, ybuf, y_s, y_r, c)
            y = times(y, all_n[c]) + both_of(ubuf, c)

        @pl.when(half == 0)
        def _():
            csend[0] = y.astype(BF16)
            c_copy.start()

        take(ysend, ybuf, y_s, y_r)
        corr[...] = cbuf[RELAX].astype(F32) + ybuf[...].astype(F32)

    @pl.when(core == 1)
    def _():
        t_copy.wait_recv()
        take(ysend, ybuf, y_s, y_r)
        corr[...] = (
            cbuf[RELAX].astype(F32) + tpair[...].astype(F32) + times(ybuf[...].astype(F32), pair_d[...])
        )

    def given(src, dst, ss, rs):
        for c in range(span):
            y_copy(src, dst, ss, rs, c, 1).wait_send()
            pl.when(lane != c)(y_copy(src, dst, ss, rs, c, 0).wait_send)

    def scan_sent():
        t_copy.wait_send()
        given(ysend, ybuf, y_s, y_r)
        pl.when(half == 0)(c_copy.wait_send)

    on(core == 0, scan_sent)

    steps = ((nz // 2, nz - 1 - nz // 2), (nz - 1 - nz // 2, nz // 2))
    most = nz // 2

    def ring_copy(r, way, s):
        slot = (z - s + nz) % nz if way == 0 else (z + s) % nz
        to = (z + 1) % nz if way == 0 else (z + nz - 1) % nz
        return remote(rbuf.at[r, slot], rbuf.at[r, slot], ring_s.at[r, way, s], ring_r.at[r, way, s], dp=x * nz + to)

    def ring_slot(way, s):
        return (z - s - 1 + nz) % nz if way == 0 else (z + s + 1) % nz

    def ring_arrival(r, way, s):
        slot = ring_slot(way, s)
        to = (z + 1) % nz if way == 0 else (z + nz - 1) % nz
        return remote(rbuf.at[r, slot], rbuf.at[r, slot], ring_s.at[r, way, s], ring_r.at[r, way, s], dp=x * nz + to)

    def ring_begin(r):
        pending.append(lambda: ring_end(r))
        for way in range(2):
            if steps[r % 2][way] > 0:
                ring_copy(r, way, 0).start()

    def ring_step(r, s):
        for way in range(2):
            if s < steps[r % 2][way]:
                ring_arrival(r, way, s).wait_recv()
                if s + 1 < steps[r % 2][way]:
                    ring_copy(r, way, s + 1).start()

    def ring_end(r):
        for way in range(2):
            for s in range(steps[r % 2][way]):
                ring_copy(r, way, s).wait_send()

    def prepare(layer, j):
        normed = rbuf[layer, j]
        norm_t[layer, j] = normed.T
        pre = nn(normed, wus[layer])
        s = sigmoid(pre)
        hid_t[layer, j] = (pre * s).astype(BF16).T
        slope_s[layer, j] = s * (1.0 + pre * (1.0 - s))

    def gather_step(s):
        for layer in range(L):
            ring_step(layer, s)

    v = corr[...]
    for layer in range(L):
        v = forward(v, layer, True)
        ring_begin(layer)

    def a_copy(s):
        return remote(asend.at[s], abuf.at[s + 1], a_s.at[s], a_r.at[s], depth=(k + nd - 1) % nd)

    abuf[0] = cot[...]

    for s in range(RELAX):
        g = abuf[s].astype(F32)
        for layer in reversed(range(L)):
            g = adjoint(g, layer)
        asend[s] = g.astype(BF16)

        @pl.when(k > 0)
        def _():
            a_copy(s).start()

        if s < most:
            gather_step(s)

        @pl.when(k < nd - 1)
        def _():
            a_copy(s).wait_recv()

        @pl.when(k == nd - 1)
        def _():
            abuf[s + 1] = abuf[0]

    on(k > 0, lambda: each(0, RELAX, lambda s: a_copy(s).wait_send()))

    b_copy = remote(bsend, bpair, b_s, b_r, depth=k + 1 - 2 * core)

    def w_copy(c):
        return remote(wsend.at[rows_of(c)], wbuf.at[core, lane], w_s.at[c], w_r.at[core, lane], depth=2 * (half * span + c))

    def w_arrival(j, c):
        return remote(wsend.at[rows_of(c)], wbuf.at[j, c], w_s.at[c], w_r.at[j, c], depth=2 * (half * span + c))

    change = abuf[RELAX].astype(F32) - abuf[RELAX - 1].astype(F32)

    @pl.when(core == 1)
    def _():
        wsend[...] = times_t(change, all_n[lane]).astype(BF16)

    @pl.when(core == 0)
    def _():
        wsend[...] = times_t(change, own_d[...]).astype(BF16)

    spread(wsend, wbuf, w_copy)
    pending.append(lambda: spread_sent(w_copy))

    @pl.when(core == 1)
    def _():
        bsend[...] = times_t(change, own_d[...]).astype(BF16)
        b_copy.start()

    for s in range(RELAX, most):
        gather_step(s)

    @pl.when(core == 0)
    def _():
        collect(w_arrival)

        @pl.when(half == 1)
        def _():
            crecv[1] = jnp.zeros((Q, D), BF16)

        @pl.when(half == 0)
        def _():
            c_back.wait_recv()

        y = crecv[1].astype(F32)
        for c in reversed(range(span)):
            zsend[c] = y.astype(BF16)
            give(zsend, zbuf, z_s, z_r, c)
            y = times_t(y, all_n[c]) + both_of(wbuf, c)

        @pl.when(half == 1)
        def _():
            csend[1] = y.astype(BF16)
            c_back.start()

    def prepare_slot(j):
        for layer in range(L):
            prepare(layer, j)

    each(0, nz, prepare_slot)

    @pl.when(core == 0)
    def _():
        b_copy.wait_recv()
        take(zsend, zbuf, z_s, z_r)
        corr[...] = (
            abuf[RELAX].astype(F32) + bpair[...].astype(F32) + times_t(zbuf[...].astype(F32), pair_d[...])
        )

    @pl.when(core == 1)
    def _():
        take(zsend, zbuf, z_s, z_r)
        corr[...] = abuf[RELAX].astype(F32) + zbuf[...].astype(F32)

    def w_sent():
        given(zsend, zbuf, z_s, z_r)
        pl.when(half == 1)(c_back.wait_send)

    on(core == 0, w_sent)
    on(core == 1, b_copy.wait_send)

    g = corr[...]
    rbuf[L + 1, z] = g.astype(BF16)
    ring_begin(L + 1)
    g = adjoint(g, 1)
    rbuf[L, z] = g.astype(BF16)
    ring_begin(L)

    gu[...] = jnp.zeros_like(gu)
    gd[...] = jnp.zeros_like(gd)

    def contract(layer, j):
        low = rbuf[L + layer, j]
        delta = (nt(low, wds[layer]) * slope_s[layer, j]).astype(BF16)
        gu[layer] += nn(norm_t[layer, j], delta)
        gd[layer] += nn(hid_t[layer, j], low)

    rows = D // ndp

    def h_copy(layer):
        return remote(
            gds.at[layer, pl.ds(pl.multiple_of((1 - x) * F, F), F)], gdrecv.at[layer],
            h_s.at[layer], h_r.at[layer], dp=(1 - x) * nz + z,
        )

    def g_copy(layer, i):
        t = (p + i) % ndp
        return remote(
            gus.at[layer, pl.ds(pl.multiple_of(t * rows, rows), rows)], gurecv.at[layer, p],
            g_s.at[layer, i], g_r.at[layer, p], dp=t,
        )

    def g_arrival(layer, i):
        t = (p + i) % ndp
        return remote(
            gus.at[layer, pl.ds(pl.multiple_of(t * rows, rows), rows)], gurecv.at[layer, t],
            g_s.at[layer, i], g_r.at[layer, t], dp=t,
        )

    def send_sums(layer):
        gds[layer] = gd[layer].astype(BF16)
        h_copy(layer).start()
        gus[layer] = gu[layer].astype(BF16)
        each(1, ndp, lambda i: g_copy(layer, i).start())
        gurecv[layer, p] = gus[layer, pl.ds(pl.multiple_of(p * rows, rows), rows), :]
        pending.append(h_copy(layer).wait_send)
        pending.append(lambda: each(1, ndp, lambda i: g_copy(layer, i).wait_send()))

    contract(1, z)
    contract(0, z)
    for s in range(most + 1):
        turns = [(layer, at) for layer, at in ((1, s), (0, s - 1)) if 0 <= at < most]
        for layer, at in turns:
            ring_step(L + layer, at)
        for layer, at in turns:
            for way in range(2):
                if at < steps[layer][way]:
                    contract(layer, ring_slot(way, at))
            if at == most - 1:
                send_sums(layer)

    for layer in (1, 0):
        h_copy(layer).wait_recv()
        gd_out[layer] = (
            gd[layer, pl.ds(pl.multiple_of(x * F, F), F), :] + gdrecv[layer].astype(F32)
        ).astype(BF16)
        each(1, ndp, lambda i: g_arrival(layer, i).wait_recv())
        for j in range(nz):
            both = (gurecv[layer, j].astype(F32) + gurecv[layer, nz + j].astype(F32)).astype(BF16)
            gu_out[layer, :, j * F:(j + 1) * F] = both[:, :F]
            gu_out[layer, :, FF // 2 + j * F:FF // 2 + (j + 1) * F] = both[:, F:]

    for wait in pending:
        wait()


def widen(up, down, up_out, down_out):
    up_out[...] = up[...].astype(F32)
    down_out[...] = down[...].astype(F32)


def shards(nd, ndp, token_ids, embedding, w_up, w_down, cotangent):
    T, D = cotangent.shape
    L, _, FF = w_up.shape
    nz, nchip = ndp // 2, nd // 2
    span = max(nchip // 2, 1)
    R, Q, F = T // nchip, T // span, FF // ndp
    most = max(nz // 2, 1)
    V = pltpu.VMEM
    sem = pltpu.SemaphoreType.DMA
    scratch = [
        V((L, D, FF), BF16), V((L, FF, D), BF16), V(embedding.shape, BF16),
        V((nd, R, D // 2), BF16), V((nd, R, D // 2), BF16), V((nd, R, D // 2), BF16),
        V((D, D), BF16), V((D, D), BF16), V((span, D, D), BF16),
        V((RELAX + 1, T, D), BF16), V((RELAX, T, D), BF16), V((RELAX + 1, T, D), BF16), V((RELAX, T, D), BF16),
        V((T, D), BF16), V((T, D), BF16), V((T, D), BF16), V((2, span, Q, D), BF16), V((span, Q, D), BF16), V((T, D), BF16),
        V((T, D), BF16), V((T, D), BF16), V((T, D), BF16), V((2, span, Q, D), BF16), V((span, Q, D), BF16), V((T, D), BF16),
        V((T, D), F32), V((L, T, D), F32), V((L, T, 1), F32), V((L, T, FF), F32),
        V((2 * L, nz, T, D), BF16), V((L, D, 2 * F), BF16), V((L, 2 * F, D), BF16),
        V((L, nz, D, T), BF16), V((L, nz, 2 * F, T), BF16), V((L, nz, T, 2 * F), F32),
        V((L, D, 2 * F), F32), V((L, 2 * F, D), F32), V((L, D, 2 * F), BF16), V((L, 2 * F, D), BF16),
        V((L, ndp, D // ndp, 2 * F), BF16), V((L, F, D), BF16),
        V((2, Q, D), BF16), V((2, Q, D), BF16),
        sem((3,)), sem((nd,)), sem((nd,)), sem((nd,)), sem((nd,)), sem, sem, sem((nchip,)), sem((nchip,)),
        sem((RELAX,)), sem((RELAX,)), sem((RELAX,)), sem((RELAX,)),
        sem, sem, sem((nchip,)), sem((2, nchip)), sem((nchip, 2)), sem((nchip,)),
        sem, sem, sem((nchip,)), sem((2, nchip)), sem((nchip, 2)), sem((nchip,)),
        sem((2 * L, 2, most)), sem((2 * L, 2, most)), sem((L, ndp)), sem((L, ndp)), sem((L,)), sem((L,)), sem((2,)), sem((2,)),
    ]
    vmem = pl.BlockSpec(memory_space=pltpu.VMEM)
    hbm = pl.BlockSpec(memory_space=pl.ANY)
    grad_up, grad_down = pl.pallas_call(
        functools.partial(kernel, nd, nz),
        out_shape=(
            jax.ShapeDtypeStruct((L, D // ndp, FF), BF16),
            jax.ShapeDtypeStruct((L, FF // ndp, D), BF16),
        ),
        in_specs=[vmem, hbm, hbm, hbm, vmem],
        out_specs=(vmem, vmem),
        scratch_shapes=scratch,
        compiler_params=pltpu.CompilerParams(
            collective_id=0, has_side_effects=True, vmem_limit_bytes=58 * 1024 * 1024
        ),
    )(token_ids[None, :], embedding, w_up, w_down, cotangent)
    return pl.pallas_call(
        widen,
        out_shape=(
            jax.ShapeDtypeStruct(grad_up.shape, F32),
            jax.ShapeDtypeStruct(grad_down.shape, F32),
        ),
        in_specs=[vmem, vmem],
        out_specs=(vmem, vmem),
    )(grad_up, grad_down)


def solution(mesh):
    in_specs = (
        P("dp"),
        P("depth", None),
        P("depth", None, None),
        P("depth", None, None),
        P("dp", None),
    )
    out_specs = (P("depth", "dp", None), P("depth", "dp", None))
    body = functools.partial(shards, mesh.shape["depth"], mesh.shape["dp"])
    return jax.shard_map(body, mesh=mesh, in_specs=in_specs, out_specs=out_specs, check_vma=False)
```

```python
import functools

import jax
import jax.numpy as jnp
from jax import lax
from jax.experimental import pallas as pl
from jax.experimental.pallas import tpu as pltpu
from jax.sharding import PartitionSpec as P

RELAX = 3
EPSILON = 1e-06
GAMMA = 0.05
F32, BF16 = jnp.float32, jnp.bfloat16
MESH = pl.DeviceIdType.MESH


def nn(a, b):
    return jnp.dot(a, b, preferred_element_type=F32)


def nt(a, b):
    return lax.dot_general(a, b, (((1,), (1,)), ((), ())), preferred_element_type=F32)


def sigmoid(p):
    return 0.5 * jnp.tanh(0.5 * p) + 0.5


def kernel(
    nd, nz,
    tok, emb_hbm, wu_hbm, wd_hbm, cot,
    gu_out, gd_out,
    wu, wd, emb,
    epick, erecv, estart,
    own_d, pair_d, all_n,
    cbuf, fsend, abuf, asend,
    tsend, tpair, usend, ubuf, ysend, ybuf,
    bsend, bpair, wsend, wbuf, zsend, zbuf,
    corr, unit, scales, slope,
    rbuf, wus, wds, norm_t, hid_t, slope_s,
    gu, gd, gus, gds, gurecv, gdrecv, csend, crecv,
    load_sem, e_s, e_r, e2_s, e2_r, d_s, d_r, n_s, n_r,
    f_s, f_r, a_s, a_r, t_s, t_r, u_s, u_r, y_s, y_r,
    b_s, b_r, w_s, w_r, z_s, z_r, ring_s, ring_r, g_s, g_r, h_s, h_r, c_s, c_r,
):
    T, D = cot.shape
    L, _, FF = wu.shape
    ndp, nchip = 2 * nz, nd // 2
    k, p = lax.axis_index("depth"), lax.axis_index("dp")
    core, chip = k % 2, k // 2
    span = max(nchip // 2, 1)
    half, lane = chip // span, chip % span
    Q = T // span
    x, z = p // nz, p % nz
    F = FF // ndp
    vocab = emb.shape[0]
    wide = min(512, FF)

    def remote(src, dst, ssem, rsem, depth=k, dp=p):
        return pltpu.make_async_remote_copy(
            src_ref=src, dst_ref=dst, send_sem=ssem, recv_sem=rsem,
            device_id={"depth": depth, "dp": dp}, device_id_type=MESH,
        )

    load_up = pltpu.make_async_copy(wu_hbm, wu, load_sem.at[0])
    load_down = pltpu.make_async_copy(wd_hbm, wd, load_sem.at[1])
    load_rows = pltpu.make_async_copy(emb_hbm, emb, load_sem.at[2])
    load_rows.start()
    load_up.start()
    load_down.start()

    barrier = pltpu.get_barrier_semaphore()
    pending = []

    def greet_depth(i, c):
        pl.semaphore_signal(barrier, inc=1, device_id={"depth": (k + i) % nd, "dp": p}, device_id_type=MESH)
        return c

    def greet_dp(i, c):
        pl.semaphore_signal(barrier, inc=1, device_id={"depth": k, "dp": (p + i) % ndp}, device_id_type=MESH)
        return c

    lax.fori_loop(1, nd, greet_depth, 0)
    lax.fori_loop(1, ndp, greet_dp, 0)

    R, H = T // nchip, D // 2
    load_rows.wait()
    local = jnp.broadcast_to(tok[...] - k * vocab, (T, T)).T[:, :1]
    onehot = (local == lax.broadcasted_iota(jnp.int32, (T, vocab), 1)).astype(BF16)
    picked = nn(onehot, emb[...]).astype(BF16)
    for c in range(nd):
        epick[c] = picked[(c // 2) * R:(c // 2 + 1) * R, (c % 2) * H:(c % 2 + 1) * H]
    pl.semaphore_wait(barrier, nd + ndp - 2)

    def pick_copy(i):
        t = (k + i) % nd
        return remote(epick.at[t], erecv.at[k], e_s.at[i], e_r.at[k], depth=t)

    def pick_arrival(i):
        t = (k + i) % nd
        return remote(epick.at[t], erecv.at[t], e_s.at[i], e_r.at[t], depth=t)

    def start_copy(i):
        t = (k + i) % nd
        return remote(estart.at[k], estart.at[k], e2_s.at[i], e2_r.at[k], depth=t)

    def start_arrival(i):
        t = (k + i) % nd
        return remote(estart.at[t], estart.at[t], e2_s.at[i], e2_r.at[t], depth=t)

    def each(low, high, f):
        def body(i, c):
            f(i)
            return c
        lax.fori_loop(low, high, body, 0)

    each(1, nd, lambda i: pick_copy(i).start())
    pending.append(lambda: each(1, nd, lambda i: pick_copy(i).wait_send()))
    erecv[k] = epick[k]

    load_up.wait()
    load_down.wait()

    def coarse_rows(i):
        rows = pl.ds(pl.multiple_of(i * 128, 128), 128)
        total = nn(wu[0, rows, :], wd[0])
        total = total + nn(wu[1, rows, :], wd[1])
        own_d[rows, :] = (GAMMA * total).astype(BF16)

    each(0, D // 128, coarse_rows)
    d_copy = remote(own_d, pair_d, d_s, d_r, depth=k + 1 - 2 * core)
    d_copy.start()
    pending.append(d_copy.wait_send)

    each(1, nd, lambda i: pick_arrival(i).wait_recv())
    total = erecv[0].astype(F32)
    for c in range(1, nd):
        total = total + erecv[c].astype(F32)
    estart[k] = total.astype(BF16)
    each(1, nd, lambda i: start_copy(i).start())
    pending.append(lambda: each(1, nd, lambda i: start_copy(i).wait_send()))

    d_copy.wait_recv()

    def n_copy(i):
        t = (lane + i) % span
        return remote(all_n.at[lane], all_n.at[lane], n_s.at[i], n_r.at[lane], depth=2 * (half * span + t))

    def n_arrival(i):
        t = (lane + i) % span
        return remote(all_n.at[t], all_n.at[t], n_s.at[i], n_r.at[t], depth=2 * (half * span + t))

    def combine(first, second):
        product = nn(first[...], second[...])
        all_n[lane] = (product + first[...].astype(F32) + second[...].astype(F32)).astype(BF16)

    @pl.when(core == 1)
    def _():
        combine(pair_d, own_d)

    @pl.when(core == 0)
    def _():
        combine(own_d, pair_d)
        each(1, span, lambda i: n_copy(i).start())

    def on(condition, f):
        pending.append(lambda: pl.when(condition)(f))

    on(core == 0, lambda: each(1, span, lambda i: n_copy(i).wait_send()))

    for piece in range(2):
        at = pl.multiple_of(piece * (FF // 2) + z * F, 128)
        for layer in range(L):
            wus[layer, :, piece * F:(piece + 1) * F] = wu[layer, :, pl.ds(at, F)]
            wds[layer, piece * F:(piece + 1) * F, :] = wd[layer, pl.ds(at, F), :]

    each(1, nd, lambda i: start_arrival(i).wait_recv())
    for c in range(nd):
        cbuf[0, (c // 2) * R:(c // 2 + 1) * R, (c % 2) * H:(c % 2 + 1) * H] = estart[c]

    def forward(v, layer, save):
        scale = lax.rsqrt(jnp.mean(v * v, axis=-1, keepdims=True) + EPSILON)
        n = v * scale
        normed = n.astype(BF16)
        if save:
            unit[layer] = n
            scales[layer] = scale
            rbuf[layer, z] = normed
        total = None
        for at in range(0, FF, wide):
            pre = nn(normed, wu[layer, :, at:at + wide])
            s = sigmoid(pre)
            if save:
                slope[layer, :, at:at + wide] = s * (1.0 + pre * (1.0 - s))
            part = nn((pre * s).astype(BF16), wd[layer, at:at + wide, :])
            total = part if total is None else total + part
        return v + total

    def adjoint(g, layer):
        low = g.astype(BF16)
        q = None
        for at in range(0, FF, wide):
            toward = nt(low, wd[layer, at:at + wide, :])
            delta = (toward * slope[layer, :, at:at + wide]).astype(BF16)
            part = nt(delta, wu[layer, :, at:at + wide])
            q = part if q is None else q + part
        n = unit[layer]
        inner = jnp.mean(q * n, axis=-1, keepdims=True)
        return g + scales[layer] * (q - n * inner)

    def f_copy(s):
        return remote(fsend.at[s], cbuf.at[s + 1], f_s.at[s], f_r.at[s], depth=(k + 1) % nd)

    def forward_sweep(s):
        v = cbuf[s].astype(F32)
        for layer in range(L):
            v = forward(v, layer, False)
        fsend[s] = v.astype(BF16)

        @pl.when(k < nd - 1)
        def _():
            f_copy(s).start()

        @pl.when(k > 0)
        def _():
            f_copy(s).wait_recv()

        @pl.when(k == 0)
        def _():
            cbuf[s + 1] = cbuf[0]

    each(0, RELAX, forward_sweep)
    on(k < nd - 1, lambda: each(0, RELAX, lambda s: f_copy(s).wait_send()))

    def times(v, d):
        return v + nn(v.astype(BF16), d)

    def times_t(v, d):
        return v + nt(v.astype(BF16), d)

    t_copy = remote(tsend, tpair, t_s, t_r, depth=k + 1 - 2 * core)

    def rows_of(c):
        return pl.ds(c * Q, Q)

    def u_copy(c):
        return remote(usend.at[rows_of(c)], ubuf.at[core, lane], u_s.at[c], u_r.at[core, lane], depth=2 * (half * span + c))

    def u_arrival(j, c):
        return remote(usend.at[rows_of(c)], ubuf.at[j, c], u_s.at[c], u_r.at[j, c], depth=2 * (half * span + c))

    def spread(src, dst, copy):
        for c in range(span):
            @pl.when((core == 1) | (lane != c))
            def _(c=c):
                copy(c).start()

            @pl.when((core == 0) & (lane == c))
            def _(c=c):
                dst[0, c] = src[rows_of(c), :]

    def collect(arrival):
        for c in range(span):
            arrival(1, c).wait_recv()

            @pl.when(lane != c)
            def _(c=c):
                arrival(0, c).wait_recv()

    def spread_sent(copy):
        for c in range(span):
            pl.when((core == 1) | (lane != c))(copy(c).wait_send)

    def both_of(buf, c):
        return buf[0, c].astype(F32) + buf[1, c].astype(F32)

    mine = pl.ds(pl.multiple_of(lane * Q, Q), Q)

    def y_copy(src, dst, ss, rs, c, to):
        return remote(src.at[c], dst.at[mine], ss.at[c, to], rs.at[lane], depth=2 * (half * span + c) + to)

    def y_arrival(src, dst, ss, rs, c):
        return remote(src.at[c], dst.at[rows_of(c)], ss.at[c, 0], rs.at[c], depth=2 * (half * span + c))

    def give(src, dst, ss, rs, c):
        y_copy(src, dst, ss, rs, c, 1).start()

        @pl.when(lane != c)
        def _():
            y_copy(src, dst, ss, rs, c, 0).start()

        @pl.when(lane == c)
        def _():
            dst[mine, :] = src[c]

    def take(src, dst, ss, rs):
        for c in range(span):
            @pl.when((core == 1) | (lane != c))
            def _(c=c):
                y_arrival(src, dst, ss, rs, c).wait_recv()

    across = (k + nchip) % nd
    c_copy = remote(csend.at[0], crecv.at[0], c_s.at[0], c_r.at[0], depth=across)
    c_back = remote(csend.at[1], crecv.at[1], c_s.at[1], c_r.at[1], depth=across)

    change = cbuf[RELAX].astype(F32) - cbuf[RELAX - 1].astype(F32)

    @pl.when(core == 0)
    def _():
        usend[...] = times(change, all_n[lane]).astype(BF16)

    @pl.when(core == 1)
    def _():
        usend[...] = times(change, own_d[...]).astype(BF16)

    spread(usend, ubuf, u_copy)
    pending.append(lambda: spread_sent(u_copy))

    @pl.when(core == 0)
    def _():
        tsend[...] = times(change, own_d[...]).astype(BF16)
        t_copy.start()
        each(1, span, lambda i: n_arrival(i).wait_recv())
        collect(u_arrival)

        @pl.when(half == 0)
        def _():
            crecv[0] = jnp.zeros((Q, D), BF16)

        @pl.when(half == 1)
        def _():
            c_copy.wait_recv()

        y = crecv[0].astype(F32)
        for c in range(span):
            ysend[c] = y.astype(BF16)
            give(ysend, ybuf, y_s, y_r, c)
            y = times(y, all_n[c]) + both_of(ubuf, c)

        @pl.when(half == 0)
        def _():
            csend[0] = y.astype(BF16)
            c_copy.start()

        take(ysend, ybuf, y_s, y_r)
        corr[...] = cbuf[RELAX].astype(F32) + ybuf[...].astype(F32)

    @pl.when(core == 1)
    def _():
        t_copy.wait_recv()
        take(ysend, ybuf, y_s, y_r)
        corr[...] = (
            cbuf[RELAX].astype(F32) + tpair[...].astype(F32) + times(ybuf[...].astype(F32), pair_d[...])
        )

    def given(src, dst, ss, rs):
        for c in range(span):
            y_copy(src, dst, ss, rs, c, 1).wait_send()
            pl.when(lane != c)(y_copy(src, dst, ss, rs, c, 0).wait_send)

    def scan_sent():
        t_copy.wait_send()
        given(ysend, ybuf, y_s, y_r)
        pl.when(half == 0)(c_copy.wait_send)

    on(core == 0, scan_sent)

    steps = ((nz // 2, nz - 1 - nz // 2), (nz - 1 - nz // 2, nz // 2))
    most = nz // 2

    def ring_copy(r, way, s):
        slot = (z - s + nz) % nz if way == 0 else (z + s) % nz
        to = (z + 1) % nz if way == 0 else (z + nz - 1) % nz
        return remote(rbuf.at[r, slot], rbuf.at[r, slot], ring_s.at[r, way, s], ring_r.at[r, way, s], dp=x * nz + to)

    def ring_slot(way, s):
        return (z - s - 1 + nz) % nz if way == 0 else (z + s + 1) % nz

    def ring_arrival(r, way, s):
        slot = ring_slot(way, s)
        to = (z + 1) % nz if way == 0 else (z + nz - 1) % nz
        return remote(rbuf.at[r, slot], rbuf.at[r, slot], ring_s.at[r, way, s], ring_r.at[r, way, s], dp=x * nz + to)

    def ring_begin(r):
        pending.append(lambda: ring_end(r))
        for way in range(2):
            if steps[r % 2][way] > 0:
                ring_copy(r, way, 0).start()

    def ring_step(r, s):
        for way in range(2):
            if s < steps[r % 2][way]:
                ring_arrival(r, way, s).wait_recv()
                if s + 1 < steps[r % 2][way]:
                    ring_copy(r, way, s + 1).start()

    def ring_end(r):
        for way in range(2):
            for s in range(steps[r % 2][way]):
                ring_copy(r, way, s).wait_send()

    def prepare(layer, j):
        normed = rbuf[layer, j]
        norm_t[layer, j] = normed.T
        pre = nn(normed, wus[layer])
        s = sigmoid(pre)
        hid_t[layer, j] = (pre * s).astype(BF16).T
        slope_s[layer, j] = s * (1.0 + pre * (1.0 - s))

    def gather_step(s):
        for layer in range(L):
            ring_step(layer, s)

    v = corr[...]
    for layer in range(L):
        v = forward(v, layer, True)
        ring_begin(layer)

    def a_copy(s):
        return remote(asend.at[s], abuf.at[s + 1], a_s.at[s], a_r.at[s], depth=(k + nd - 1) % nd)

    abuf[0] = cot[...]

    for s in range(RELAX):
        g = abuf[s].astype(F32)
        for layer in reversed(range(L)):
            g = adjoint(g, layer)
        asend[s] = g.astype(BF16)

        @pl.when(k > 0)
        def _():
            a_copy(s).start()

        if s < most:
            gather_step(s)

        @pl.when(k < nd - 1)
        def _():
            a_copy(s).wait_recv()

        @pl.when(k == nd - 1)
        def _():
            abuf[s + 1] = abuf[0]

    on(k > 0, lambda: each(0, RELAX, lambda s: a_copy(s).wait_send()))

    b_copy = remote(bsend, bpair, b_s, b_r, depth=k + 1 - 2 * core)

    def w_copy(c):
        return remote(wsend.at[rows_of(c)], wbuf.at[core, lane], w_s.at[c], w_r.at[core, lane], depth=2 * (half * span + c))

    def w_arrival(j, c):
        return remote(wsend.at[rows_of(c)], wbuf.at[j, c], w_s.at[c], w_r.at[j, c], depth=2 * (half * span + c))

    change = abuf[RELAX].astype(F32) - abuf[RELAX - 1].astype(F32)

    @pl.when(core == 1)
    def _():
        wsend[...] = times_t(change, all_n[lane]).astype(BF16)

    @pl.when(core == 0)
    def _():
        wsend[...] = times_t(change, own_d[...]).astype(BF16)

    spread(wsend, wbuf, w_copy)
    pending.append(lambda: spread_sent(w_copy))

    @pl.when(core == 1)
    def _():
        bsend[...] = times_t(change, own_d[...]).astype(BF16)
        b_copy.start()

    for s in range(RELAX, most):
        gather_step(s)

    @pl.when(core == 0)
    def _():
        collect(w_arrival)

        @pl.when(half == 1)
        def _():
            crecv[1] = jnp.zeros((Q, D), BF16)

        @pl.when(half == 0)
        def _():
            c_back.wait_recv()

        y = crecv[1].astype(F32)
        for c in reversed(range(span)):
            zsend[c] = y.astype(BF16)
            give(zsend, zbuf, z_s, z_r, c)
            y = times_t(y, all_n[c]) + both_of(wbuf, c)

        @pl.when(half == 1)
        def _():
            csend[1] = y.astype(BF16)
            c_back.start()

    def prepare_slot(j):
        for layer in range(L):
            prepare(layer, j)

    each(0, nz, prepare_slot)

    @pl.when(core == 0)
    def _():
        b_copy.wait_recv()
        take(zsend, zbuf, z_s, z_r)
        corr[...] = (
            abuf[RELAX].astype(F32) + bpair[...].astype(F32) + times_t(zbuf[...].astype(F32), pair_d[...])
        )

    @pl.when(core == 1)
    def _():
        take(zsend, zbuf, z_s, z_r)
        corr[...] = abuf[RELAX].astype(F32) + zbuf[...].astype(F32)

    def w_sent():
        given(zsend, zbuf, z_s, z_r)
        pl.when(half == 1)(c_back.wait_send)

    on(core == 0, w_sent)
    on(core == 1, b_copy.wait_send)

    g = corr[...]
    rbuf[L + 1, z] = g.astype(BF16)
    ring_begin(L + 1)
    g = adjoint(g, 1)
    rbuf[L, z] = g.astype(BF16)
    ring_begin(L)

    gu[...] = jnp.zeros_like(gu)
    gd[...] = jnp.zeros_like(gd)

    def contract(layer, j):
        low = rbuf[L + layer, j]
        delta = (nt(low, wds[layer]) * slope_s[layer, j]).astype(BF16)
        gu[layer] += nn(norm_t[layer, j], delta)
        gd[layer] += nn(hid_t[layer, j], low)

    rows = D // ndp

    def h_copy(layer):
        return remote(
            gds.at[layer, pl.ds(pl.multiple_of((1 - x) * F, F), F)], gdrecv.at[layer],
            h_s.at[layer], h_r.at[layer], dp=(1 - x) * nz + z,
        )

    def g_copy(layer, i):
        t = (p + i) % ndp
        return remote(
            gus.at[layer, pl.ds(pl.multiple_of(t * rows, rows), rows)], gurecv.at[layer, p],
            g_s.at[layer, i], g_r.at[layer, p], dp=t,
        )

    def g_arrival(layer, i):
        t = (p + i) % ndp
        return remote(
            gus.at[layer, pl.ds(pl.multiple_of(t * rows, rows), rows)], gurecv.at[layer, t],
            g_s.at[layer, i], g_r.at[layer, t], dp=t,
        )

    def send_sums(layer):
        gds[layer] = gd[layer].astype(BF16)
        h_copy(layer).start()
        gus[layer] = gu[layer].astype(BF16)
        each(1, ndp, lambda i: g_copy(layer, i).start())
        gurecv[layer, p] = gus[layer, pl.ds(pl.multiple_of(p * rows, rows), rows), :]
        pending.append(h_copy(layer).wait_send)
        pending.append(lambda: each(1, ndp, lambda i: g_copy(layer, i).wait_send()))

    contract(1, z)
    contract(0, z)
    for s in range(most + 1):
        turns = [(layer, at) for layer, at in ((1, s), (0, s - 1)) if 0 <= at < most]
        for layer, at in turns:
            ring_step(L + layer, at)
        for layer, at in turns:
            for way in range(2):
                if at < steps[layer][way]:
                    contract(layer, ring_slot(way, at))
            if at == most - 1:
                send_sums(layer)

    for layer in (1, 0):
        h_copy(layer).wait_recv()
        gd_out[layer] = (
            gd[layer, pl.ds(pl.multiple_of(x * F, F), F), :] + gdrecv[layer].astype(F32)
        ).astype(BF16)
        each(1, ndp, lambda i: g_arrival(layer, i).wait_recv())
        for j in range(nz):
            both = (gurecv[layer, j].astype(F32) + gurecv[layer, nz + j].astype(F32)).astype(BF16)
            gu_out[layer, :, j * F:(j + 1) * F] = both[:, :F]
            gu_out[layer, :, FF // 2 + j * F:FF // 2 + (j + 1) * F] = both[:, F:]

    for wait in pending:
        wait()


def widen(up, down, up_out, down_out):
    up_out[...] = up[...].astype(F32)
    down_out[...] = down[...].astype(F32)


def shards(nd, ndp, token_ids, embedding, w_up, w_down, cotangent):
    T, D = cotangent.shape
    L, _, FF = w_up.shape
    nz, nchip = ndp // 2, nd // 2
    span = max(nchip // 2, 1)
    R, Q, F = T // nchip, T // span, FF // ndp
    most = max(nz // 2, 1)
    V = pltpu.VMEM
    sem = pltpu.SemaphoreType.DMA
    scratch = [
        V((L, D, FF), BF16), V((L, FF, D), BF16), V(embedding.shape, BF16),
        V((nd, R, D // 2), BF16), V((nd, R, D // 2), BF16), V((nd, R, D // 2), BF16),
        V((D, D), BF16), V((D, D), BF16), V((span, D, D), BF16),
        V((RELAX + 1, T, D), BF16), V((RELAX, T, D), BF16), V((RELAX + 1, T, D), BF16), V((RELAX, T, D), BF16),
        V((T, D), BF16), V((T, D), BF16), V((T, D), BF16), V((2, span, Q, D), BF16), V((span, Q, D), BF16), V((T, D), BF16),
        V((T, D), BF16), V((T, D), BF16), V((T, D), BF16), V((2, span, Q, D), BF16), V((span, Q, D), BF16), V((T, D), BF16),
        V((T, D), F32), V((L, T, D), F32), V((L, T, 1), F32), V((L, T, FF), F32),
        V((2 * L, nz, T, D), BF16), V((L, D, 2 * F), BF16), V((L, 2 * F, D), BF16),
        V((L, nz, D, T), BF16), V((L, nz, 2 * F, T), BF16), V((L, nz, T, 2 * F), F32),
        V((L, D, 2 * F), F32), V((L, 2 * F, D), F32), V((L, D, 2 * F), BF16), V((L, 2 * F, D), BF16),
        V((L, ndp, D // ndp, 2 * F), BF16), V((L, F, D), BF16),
        V((2, Q, D), BF16), V((2, Q, D), BF16),
        sem((3,)), sem((nd,)), sem((nd,)), sem((nd,)), sem((nd,)), sem, sem, sem((nchip,)), sem((nchip,)),
        sem((RELAX,)), sem((RELAX,)), sem((RELAX,)), sem((RELAX,)),
        sem, sem, sem((nchip,)), sem((2, nchip)), sem((nchip, 2)), sem((nchip,)),
        sem, sem, sem((nchip,)), sem((2, nchip)), sem((nchip, 2)), sem((nchip,)),
        sem((2 * L, 2, most)), sem((2 * L, 2, most)), sem((L, ndp)), sem((L, ndp)), sem((L,)), sem((L,)), sem((2,)), sem((2,)),
    ]
    vmem = pl.BlockSpec(memory_space=pltpu.VMEM)
    hbm = pl.BlockSpec(memory_space=pl.ANY)
    grad_up, grad_down = pl.pallas_call(
        functools.partial(kernel, nd, nz),
        out_shape=(
            jax.ShapeDtypeStruct((L, D // ndp, FF), BF16),
            jax.ShapeDtypeStruct((L, FF // ndp, D), BF16),
        ),
        in_specs=[vmem, hbm, hbm, hbm, vmem],
        out_specs=(vmem, vmem),
        scratch_shapes=scratch,
        compiler_params=pltpu.CompilerParams(
            collective_id=0, has_side_effects=True, vmem_limit_bytes=58 * 1024 * 1024
        ),
    )(token_ids[None, :], embedding, w_up, w_down, cotangent)
    return pl.pallas_call(
        widen,
        out_shape=(
            jax.ShapeDtypeStruct(grad_up.shape, F32),
            jax.ShapeDtypeStruct(grad_down.shape, F32),
        ),
        in_specs=[vmem, vmem],
        out_specs=(vmem, vmem),
    )(grad_up, grad_down)


def solution(mesh):
    in_specs = (
        P("dp"),
        P("depth", None),
        P("depth", None, None),
        P("depth", None, None),
        P("dp", None),
    )
    out_specs = (P("depth", "dp", None), P("depth", "dp", None))
    body = functools.partial(shards, mesh.shape["depth"], mesh.shape["dp"])
    return jax.shard_map(body, mesh=mesh, in_specs=in_specs, out_specs=out_specs, check_vma=False)
```

```python
import functools

import jax
import jax.numpy as jnp
from jax import lax
from jax.experimental import pallas as pl
from jax.experimental.pallas import tpu as pltpu
from jax.sharding import PartitionSpec as P

RELAX = 3
EPSILON = 1e-06
GAMMA = 0.05
F32, BF16 = jnp.float32, jnp.bfloat16
MESH = pl.DeviceIdType.MESH


def nn(a, b):
    return jnp.dot(a, b, preferred_element_type=F32)


def nt(a, b):
    return lax.dot_general(a, b, (((1,), (1,)), ((), ())), preferred_element_type=F32)


def sigmoid(p):
    return 0.5 * jnp.tanh(0.5 * p) + 0.5


def kernel(
    nd, nz,
    tok, emb_hbm, wu_hbm, wd_hbm, cot,
    gu_out, gd_out,
    wu, wd, emb,
    epick, erecv, estart,
    own_d, pair_d, all_n,
    cbuf, fsend, abuf, asend,
    tsend, tpair, usend, ubuf, ysend, ybuf,
    bsend, bpair, wsend, wbuf, zsend, zbuf,
    corr, unit, scales, slope,
    rbuf, wus, wds, norm_t, hid_t, slope_s,
    gu, gd, gus, gds, gurecv, gdrecv, csend, crecv,
    load_sem, e_s, e_r, e2_s, e2_r, d_s, d_r, n_s, n_r,
    f_s, f_r, a_s, a_r, t_s, t_r, u_s, u_r, y_s, y_r,
    b_s, b_r, w_s, w_r, z_s, z_r, ring_s, ring_r, g_s, g_r, h_s, h_r, c_s, c_r,
):
    T, D = cot.shape
    L, _, FF = wu.shape
    ndp, nchip = 2 * nz, nd // 2
    k, p = lax.axis_index("depth"), lax.axis_index("dp")
    core, chip = k % 2, k // 2
    span = max(nchip // 2, 1)
    half, lane = chip // span, chip % span
    Q = T // span
    x, z = p // nz, p % nz
    F = FF // ndp
    vocab = emb.shape[0]
    wide = min(512, FF)

    def remote(src, dst, ssem, rsem, depth=k, dp=p):
        return pltpu.make_async_remote_copy(
            src_ref=src, dst_ref=dst, send_sem=ssem, recv_sem=rsem,
            device_id={"depth": depth, "dp": dp}, device_id_type=MESH,
        )

    load_up = pltpu.make_async_copy(wu_hbm, wu, load_sem.at[0])
    load_down = pltpu.make_async_copy(wd_hbm, wd, load_sem.at[1])
    load_rows = pltpu.make_async_copy(emb_hbm, emb, load_sem.at[2])
    load_rows.start()
    load_up.start()
    load_down.start()

    barrier = pltpu.get_barrier_semaphore()
    pending = []

    def greet_depth(i, c):
        pl.semaphore_signal(barrier, inc=1, device_id={"depth": (k + i) % nd, "dp": p}, device_id_type=MESH)
        return c

    def greet_dp(i, c):
        pl.semaphore_signal(barrier, inc=1, device_id={"depth": k, "dp": (p + i) % ndp}, device_id_type=MESH)
        return c

    lax.fori_loop(1, nd, greet_depth, 0)
    lax.fori_loop(1, ndp, greet_dp, 0)

    R, H = T // nchip, D // 2
    load_rows.wait()
    local = jnp.broadcast_to(tok[...] - k * vocab, (T, T)).T[:, :1]
    onehot = (local == lax.broadcasted_iota(jnp.int32, (T, vocab), 1)).astype(BF16)
    picked = nn(onehot, emb[...]).astype(BF16)
    for c in range(nd):
        epick[c] = picked[(c // 2) * R:(c // 2 + 1) * R, (c % 2) * H:(c % 2 + 1) * H]
    pl.semaphore_wait(barrier, nd + ndp - 2)

    def pick_copy(i):
        t = (k + i) % nd
        return remote(epick.at[t], erecv.at[k], e_s.at[i], e_r.at[k], depth=t)

    def pick_arrival(i):
        t = (k + i) % nd
        return remote(epick.at[t], erecv.at[t], e_s.at[i], e_r.at[t], depth=t)

    def start_copy(i):
        t = (k + i) % nd
        return remote(estart.at[k], estart.at[k], e2_s.at[i], e2_r.at[k], depth=t)

    def start_arrival(i):
        t = (k + i) % nd
        return remote(estart.at[t], estart.at[t], e2_s.at[i], e2_r.at[t], depth=t)

    def each(low, high, f):
        def body(i, c):
            f(i)
            return c
        lax.fori_loop(low, high, body, 0)

    each(1, nd, lambda i: pick_copy(i).start())
    pending.append(lambda: each(1, nd, lambda i: pick_copy(i).wait_send()))
    erecv[k] = epick[k]

    load_up.wait()
    load_down.wait()

    def coarse_rows(i):
        rows = pl.ds(pl.multiple_of(i * 128, 128), 128)
        total = nn(wu[0, rows, :], wd[0])
        total = total + nn(wu[1, rows, :], wd[1])
        own_d[rows, :] = (GAMMA * total).astype(BF16)

    each(0, D // 128, coarse_rows)
    d_copy = remote(own_d, pair_d, d_s, d_r, depth=k + 1 - 2 * core)
    d_copy.start()
    pending.append(d_copy.wait_send)

    each(1, nd, lambda i: pick_arrival(i).wait_recv())
    total = erecv[0].astype(F32)
    for c in range(1, nd):
        total = total + erecv[c].astype(F32)
    estart[k] = total.astype(BF16)
    each(1, nd, lambda i: start_copy(i).start())
    pending.append(lambda: each(1, nd, lambda i: start_copy(i).wait_send()))

    d_copy.wait_recv()

    def n_copy(i):
        t = (lane + i) % span
        return remote(all_n.at[lane], all_n.at[lane], n_s.at[i], n_r.at[lane], depth=2 * (half * span + t))

    def n_arrival(i):
        t = (lane + i) % span
        return remote(all_n.at[t], all_n.at[t], n_s.at[i], n_r.at[t], depth=2 * (half * span + t))

    def combine(first, second):
        product = nn(first[...], second[...])
        all_n[lane] = (product + first[...].astype(F32) + second[...].astype(F32)).astype(BF16)

    @pl.when(core == 1)
    def _():
        combine(pair_d, own_d)

    @pl.when(core == 0)
    def _():
        combine(own_d, pair_d)
        each(1, span, lambda i: n_copy(i).start())

    def on(condition, f):
        pending.append(lambda: pl.when(condition)(f))

    on(core == 0, lambda: each(1, span, lambda i: n_copy(i).wait_send()))

    for piece in range(2):
        at = pl.multiple_of(piece * (FF // 2) + z * F, 128)
        for layer in range(L):
            wus[layer, :, piece * F:(piece + 1) * F] = wu[layer, :, pl.ds(at, F)]
            wds[layer, piece * F:(piece + 1) * F, :] = wd[layer, pl.ds(at, F), :]

    each(1, nd, lambda i: start_arrival(i).wait_recv())
    for c in range(nd):
        cbuf[0, (c // 2) * R:(c // 2 + 1) * R, (c % 2) * H:(c % 2 + 1) * H] = estart[c]

    def forward(v, layer, save):
        scale = lax.rsqrt(jnp.mean(v * v, axis=-1, keepdims=True) + EPSILON)
        n = v * scale
        normed = n.astype(BF16)
        if save:
            unit[layer] = n
            scales[layer] = scale
            rbuf[layer, z] = normed
        total = None
        for at in range(0, FF, wide):
            pre = nn(normed, wu[layer, :, at:at + wide])
            s = sigmoid(pre)
            if save:
                slope[layer, :, at:at + wide] = s * (1.0 + pre * (1.0 - s))
            part = nn((pre * s).astype(BF16), wd[layer, at:at + wide, :])
            total = part if total is None else total + part
        return v + total

    def adjoint(g, layer):
        low = g.astype(BF16)
        q = None
        for at in range(0, FF, wide):
            toward = nt(low, wd[layer, at:at + wide, :])
            delta = (toward * slope[layer, :, at:at + wide]).astype(BF16)
            part = nt(delta, wu[layer, :, at:at + wide])
            q = part if q is None else q + part
        n = unit[layer]
        inner = jnp.mean(q * n, axis=-1, keepdims=True)
        return g + scales[layer] * (q - n * inner)

    def f_copy(s):
        return remote(fsend.at[s], cbuf.at[s + 1], f_s.at[s], f_r.at[s], depth=(k + 1) % nd)

    def forward_sweep(s):
        v = cbuf[s].astype(F32)
        for layer in range(L):
            v = forward(v, layer, False)
        fsend[s] = v.astype(BF16)

        @pl.when(k < nd - 1)
        def _():
            f_copy(s).start()

        @pl.when(k > 0)
        def _():
            f_copy(s).wait_recv()

        @pl.when(k == 0)
        def _():
            cbuf[s + 1] = cbuf[0]

    each(0, RELAX, forward_sweep)
    on(k < nd - 1, lambda: each(0, RELAX, lambda s: f_copy(s).wait_send()))

    def times(v, d):
        return v + nn(v.astype(BF16), d)

    def times_t(v, d):
        return v + nt(v.astype(BF16), d)

    t_copy = remote(tsend, tpair, t_s, t_r, depth=k + 1 - 2 * core)

    def rows_of(c):
        return pl.ds(c * Q, Q)

    def u_copy(c):
        return remote(usend.at[rows_of(c)], ubuf.at[core, lane], u_s.at[c], u_r.at[core, lane], depth=2 * (half * span + c))

    def u_arrival(j, c):
        return remote(usend.at[rows_of(c)], ubuf.at[j, c], u_s.at[c], u_r.at[j, c], depth=2 * (half * span + c))

    def spread(src, dst, copy):
        for c in range(span):
            @pl.when((core == 1) | (lane != c))
            def _(c=c):
                copy(c).start()

            @pl.when((core == 0) & (lane == c))
            def _(c=c):
                dst[0, c] = src[rows_of(c), :]

    def collect(arrival):
        for c in range(span):
            arrival(1, c).wait_recv()

            @pl.when(lane != c)
            def _(c=c):
                arrival(0, c).wait_recv()

    def spread_sent(copy):
        for c in range(span):
            pl.when((core == 1) | (lane != c))(copy(c).wait_send)

    def both_of(buf, c):
        return buf[0, c].astype(F32) + buf[1, c].astype(F32)

    mine = pl.ds(pl.multiple_of(lane * Q, Q), Q)

    def y_copy(src, dst, ss, rs, c, to):
        return remote(src.at[c], dst.at[mine], ss.at[c, to], rs.at[lane], depth=2 * (half * span + c) + to)

    def y_arrival(src, dst, ss, rs, c):
        return remote(src.at[c], dst.at[rows_of(c)], ss.at[c, 0], rs.at[c], depth=2 * (half * span + c))

    def give(src, dst, ss, rs, c):
        y_copy(src, dst, ss, rs, c, 1).start()

        @pl.when(lane != c)
        def _():
            y_copy(src, dst, ss, rs, c, 0).start()

        @pl.when(lane == c)
        def _():
            dst[mine, :] = src[c]

    def take(src, dst, ss, rs):
        for c in range(span):
            @pl.when((core == 1) | (lane != c))
            def _(c=c):
                y_arrival(src, dst, ss, rs, c).wait_recv()

    across = (k + nchip) % nd
    c_copy = remote(csend.at[0], crecv.at[0], c_s.at[0], c_r.at[0], depth=across)
    c_back = remote(csend.at[1], crecv.at[1], c_s.at[1], c_r.at[1], depth=across)

    change = cbuf[RELAX].astype(F32) - cbuf[RELAX - 1].astype(F32)

    @pl.when(core == 0)
    def _():
        usend[...] = times(change, all_n[lane]).astype(BF16)

    @pl.when(core == 1)
    def _():
        usend[...] = times(change, own_d[...]).astype(BF16)

    spread(usend, ubuf, u_copy)
    pending.append(lambda: spread_sent(u_copy))

    @pl.when(core == 0)
    def _():
        tsend[...] = times(change, own_d[...]).astype(BF16)
        t_copy.start()
        each(1, span, lambda i: n_arrival(i).wait_recv())
        collect(u_arrival)

        @pl.when(half == 0)
        def _():
            crecv[0] = jnp.zeros((Q, D), BF16)

        @pl.when(half == 1)
        def _():
            c_copy.wait_recv()

        y = crecv[0].astype(F32)
        for c in range(span):
            ysend[c] = y.astype(BF16)
            give(ysend, ybuf, y_s, y_r, c)
            y = times(y, all_n[c]) + both_of(ubuf, c)

        @pl.when(half == 0)
        def _():
            csend[0] = y.astype(BF16)
            c_copy.start()

        take(ysend, ybuf, y_s, y_r)
        corr[...] = cbuf[RELAX].astype(F32) + ybuf[...].astype(F32)

    @pl.when(core == 1)
    def _():
        t_copy.wait_recv()
        take(ysend, ybuf, y_s, y_r)
        corr[...] = (
            cbuf[RELAX].astype(F32) + tpair[...].astype(F32) + times(ybuf[...].astype(F32), pair_d[...])
        )

    def given(src, dst, ss, rs):
        for c in range(span):
            y_copy(src, dst, ss, rs, c, 1).wait_send()
            pl.when(lane != c)(y_copy(src, dst, ss, rs, c, 0).wait_send)

    def scan_sent():
        t_copy.wait_send()
        given(ysend, ybuf, y_s, y_r)
        pl.when(half == 0)(c_copy.wait_send)

    on(core == 0, scan_sent)

    steps = ((nz // 2, nz - 1 - nz // 2), (nz - 1 - nz // 2, nz // 2))
    most = nz // 2

    def ring_copy(r, way, s):
        slot = (z - s + nz) % nz if way == 0 else (z + s) % nz
        to = (z + 1) % nz if way == 0 else (z + nz - 1) % nz
        return remote(rbuf.at[r, slot], rbuf.at[r, slot], ring_s.at[r, way, s], ring_r.at[r, way, s], dp=x * nz + to)

    def ring_slot(way, s):
        return (z - s - 1 + nz) % nz if way == 0 else (z + s + 1) % nz

    def ring_arrival(r, way, s):
        slot = ring_slot(way, s)
        to = (z + 1) % nz if way == 0 else (z + nz - 1) % nz
        return remote(rbuf.at[r, slot], rbuf.at[r, slot], ring_s.at[r, way, s], ring_r.at[r, way, s], dp=x * nz + to)

    def ring_begin(r):
        pending.append(lambda: ring_end(r))
        for way in range(2):
            if steps[r % 2][way] > 0:
                ring_copy(r, way, 0).start()

    def ring_step(r, s):
        for way in range(2):
            if s < steps[r % 2][way]:
                ring_arrival(r, way, s).wait_recv()
                if s + 1 < steps[r % 2][way]:
                    ring_copy(r, way, s + 1).start()

    def ring_end(r):
        for way in range(2):
            for s in range(steps[r % 2][way]):
                ring_copy(r, way, s).wait_send()

    def prepare(layer, j):
        normed = rbuf[layer, j]
        norm_t[layer, j] = normed.T
        pre = nn(normed, wus[layer])
        s = sigmoid(pre)
        hid_t[layer, j] = (pre * s).astype(BF16).T
        slope_s[layer, j] = s * (1.0 + pre * (1.0 - s))

    def gather_step(s):
        for layer in range(L):
            ring_step(layer, s)

    v = corr[...]
    for layer in range(L):
        v = forward(v, layer, True)
        ring_begin(layer)

    def a_copy(s):
        return remote(asend.at[s], abuf.at[s + 1], a_s.at[s], a_r.at[s], depth=(k + nd - 1) % nd)

    abuf[0] = cot[...]

    for s in range(RELAX):
        g = abuf[s].astype(F32)
        for layer in reversed(range(L)):
            g = adjoint(g, layer)
        asend[s] = g.astype(BF16)

        @pl.when(k > 0)
        def _():
            a_copy(s).start()

        if s < most:
            gather_step(s)

        @pl.when(k < nd - 1)
        def _():
            a_copy(s).wait_recv()

        @pl.when(k == nd - 1)
        def _():
            abuf[s + 1] = abuf[0]

    on(k > 0, lambda: each(0, RELAX, lambda s: a_copy(s).wait_send()))

    b_copy = remote(bsend, bpair, b_s, b_r, depth=k + 1 - 2 * core)

    def w_copy(c):
        return remote(wsend.at[rows_of(c)], wbuf.at[core, lane], w_s.at[c], w_r.at[core, lane], depth=2 * (half * span + c))

    def w_arrival(j, c):
        return remote(wsend.at[rows_of(c)], wbuf.at[j, c], w_s.at[c], w_r.at[j, c], depth=2 * (half * span + c))

    change = abuf[RELAX].astype(F32) - abuf[RELAX - 1].astype(F32)

    @pl.when(core == 1)
    def _():
        wsend[...] = times_t(change, all_n[lane]).astype(BF16)

    @pl.when(core == 0)
    def _():
        wsend[...] = times_t(change, own_d[...]).astype(BF16)

    spread(wsend, wbuf, w_copy)
    pending.append(lambda: spread_sent(w_copy))

    @pl.when(core == 1)
    def _():
        bsend[...] = times_t(change, own_d[...]).astype(BF16)
        b_copy.start()

    for s in range(RELAX, most):
        gather_step(s)

    @pl.when(core == 0)
    def _():
        collect(w_arrival)

        @pl.when(half == 1)
        def _():
            crecv[1] = jnp.zeros((Q, D), BF16)

        @pl.when(half == 0)
        def _():
            c_back.wait_recv()

        y = crecv[1].astype(F32)
        for c in reversed(range(span)):
            zsend[c] = y.astype(BF16)
            give(zsend, zbuf, z_s, z_r, c)
            y = times_t(y, all_n[c]) + both_of(wbuf, c)

        @pl.when(half == 1)
        def _():
            csend[1] = y.astype(BF16)
            c_back.start()

    def prepare_slot(j):
        for layer in range(L):
            prepare(layer, j)

    each(0, nz, prepare_slot)

    @pl.when(core == 0)
    def _():
        b_copy.wait_recv()
        take(zsend, zbuf, z_s, z_r)
        corr[...] = (
            abuf[RELAX].astype(F32) + bpair[...].astype(F32) + times_t(zbuf[...].astype(F32), pair_d[...])
        )

    @pl.when(core == 1)
    def _():
        take(zsend, zbuf, z_s, z_r)
        corr[...] = abuf[RELAX].astype(F32) + zbuf[...].astype(F32)

    def w_sent():
        given(zsend, zbuf, z_s, z_r)
        pl.when(half == 1)(c_back.wait_send)

    on(core == 0, w_sent)
    on(core == 1, b_copy.wait_send)

    g = corr[...]
    rbuf[L + 1, z] = g.astype(BF16)
    ring_begin(L + 1)
    g = adjoint(g, 1)
    rbuf[L, z] = g.astype(BF16)
    ring_begin(L)

    gu[...] = jnp.zeros_like(gu)
    gd[...] = jnp.zeros_like(gd)

    def contract(layer, j):
        low = rbuf[L + layer, j]
        delta = (nt(low, wds[layer]) * slope_s[layer, j]).astype(BF16)
        gu[layer] += nn(norm_t[layer, j], delta)
        gd[layer] += nn(hid_t[layer, j], low)

    rows = D // ndp

    def h_copy(layer):
        return remote(
            gds.at[layer, pl.ds(pl.multiple_of((1 - x) * F, F), F)], gdrecv.at[layer],
            h_s.at[layer], h_r.at[layer], dp=(1 - x) * nz + z,
        )

    def g_copy(layer, i):
        t = (p + i) % ndp
        return remote(
            gus.at[layer, pl.ds(pl.multiple_of(t * rows, rows), rows)], gurecv.at[layer, p],
            g_s.at[layer, i], g_r.at[layer, p], dp=t,
        )

    def g_arrival(layer, i):
        t = (p + i) % ndp
        return remote(
            gus.at[layer, pl.ds(pl.multiple_of(t * rows, rows), rows)], gurecv.at[layer, t],
            g_s.at[layer, i], g_r.at[layer, t], dp=t,
        )

    def send_sums(layer):
        gds[layer] = gd[layer].astype(BF16)
        h_copy(layer).start()
        gus[layer] = gu[layer].astype(BF16)
        each(1, ndp, lambda i: g_copy(layer, i).start())
        gurecv[layer, p] = gus[layer, pl.ds(pl.multiple_of(p * rows, rows), rows), :]
        pending.append(h_copy(layer).wait_send)
        pending.append(lambda: each(1, ndp, lambda i: g_copy(layer, i).wait_send()))

    contract(1, z)
    contract(0, z)
    for s in range(most):
        for layer in (1, 0):
            ring_step(L + layer, s)
        for layer in (1, 0):
            for way in range(2):
                if s < steps[layer][way]:
                    contract(layer, ring_slot(way, s))
            if s == most - 1:
                send_sums(layer)

    for layer in (1, 0):
        h_copy(layer).wait_recv()
        gd_out[layer] = (
            gd[layer, pl.ds(pl.multiple_of(x * F, F), F), :] + gdrecv[layer].astype(F32)
        ).astype(BF16)
        each(1, ndp, lambda i: g_arrival(layer, i).wait_recv())
        for j in range(nz):
            both = (gurecv[layer, j].astype(F32) + gurecv[layer, nz + j].astype(F32)).astype(BF16)
            gu_out[layer, :, j * F:(j + 1) * F] = both[:, :F]
            gu_out[layer, :, FF // 2 + j * F:FF // 2 + (j + 1) * F] = both[:, F:]

    for wait in pending:
        wait()


def widen(up, down, up_out, down_out):
    up_out[...] = up[...].astype(F32)
    down_out[...] = down[...].astype(F32)


def shards(nd, ndp, token_ids, embedding, w_up, w_down, cotangent):
    T, D = cotangent.shape
    L, _, FF = w_up.shape
    nz, nchip = ndp // 2, nd // 2
    span = max(nchip // 2, 1)
    R, Q, F = T // nchip, T // span, FF // ndp
    most = max(nz // 2, 1)
    V = pltpu.VMEM
    sem = pltpu.SemaphoreType.DMA
    scratch = [
        V((L, D, FF), BF16), V((L, FF, D), BF16), V(embedding.shape, BF16),
        V((nd, R, D // 2), BF16), V((nd, R, D // 2), BF16), V((nd, R, D // 2), BF16),
        V((D, D), BF16), V((D, D), BF16), V((span, D, D), BF16),
        V((RELAX + 1, T, D), BF16), V((RELAX, T, D), BF16), V((RELAX + 1, T, D), BF16), V((RELAX, T, D), BF16),
        V((T, D), BF16), V((T, D), BF16), V((T, D), BF16), V((2, span, Q, D), BF16), V((span, Q, D), BF16), V((T, D), BF16),
        V((T, D), BF16), V((T, D), BF16), V((T, D), BF16), V((2, span, Q, D), BF16), V((span, Q, D), BF16), V((T, D), BF16),
        V((T, D), F32), V((L, T, D), F32), V((L, T, 1), F32), V((L, T, FF), F32),
        V((2 * L, nz, T, D), BF16), V((L, D, 2 * F), BF16), V((L, 2 * F, D), BF16),
        V((L, nz, D, T), BF16), V((L, nz, 2 * F, T), BF16), V((L, nz, T, 2 * F), F32),
        V((L, D, 2 * F), F32), V((L, 2 * F, D), F32), V((L, D, 2 * F), BF16), V((L, 2 * F, D), BF16),
        V((L, ndp, D // ndp, 2 * F), BF16), V((L, F, D), BF16),
        V((2, Q, D), BF16), V((2, Q, D), BF16),
        sem((3,)), sem((nd,)), sem((nd,)), sem((nd,)), sem((nd,)), sem, sem, sem((nchip,)), sem((nchip,)),
        sem((RELAX,)), sem((RELAX,)), sem((RELAX,)), sem((RELAX,)),
        sem, sem, sem((nchip,)), sem((2, nchip)), sem((nchip, 2)), sem((nchip,)),
        sem, sem, sem((nchip,)), sem((2, nchip)), sem((nchip, 2)), sem((nchip,)),
        sem((2 * L, 2, most)), sem((2 * L, 2, most)), sem((L, ndp)), sem((L, ndp)), sem((L,)), sem((L,)), sem((2,)), sem((2,)),
    ]
    vmem = pl.BlockSpec(memory_space=pltpu.VMEM)
    hbm = pl.BlockSpec(memory_space=pl.ANY)
    grad_up, grad_down = pl.pallas_call(
        functools.partial(kernel, nd, nz),
        out_shape=(
            jax.ShapeDtypeStruct((L, D // ndp, FF), BF16),
            jax.ShapeDtypeStruct((L, FF // ndp, D), BF16),
        ),
        in_specs=[vmem, hbm, hbm, hbm, vmem],
        out_specs=(vmem, vmem),
        scratch_shapes=scratch,
        compiler_params=pltpu.CompilerParams(
            collective_id=0, has_side_effects=True, vmem_limit_bytes=58 * 1024 * 1024
        ),
    )(token_ids[None, :], embedding, w_up, w_down, cotangent)
    return pl.pallas_call(
        widen,
        out_shape=(
            jax.ShapeDtypeStruct(grad_up.shape, F32),
            jax.ShapeDtypeStruct(grad_down.shape, F32),
        ),
        in_specs=[vmem, vmem],
        out_specs=(vmem, vmem),
    )(grad_up, grad_down)


def solution(mesh):
    in_specs = (
        P("dp"),
        P("depth", None),
        P("depth", None, None),
        P("depth", None, None),
        P("dp", None),
    )
    out_specs = (P("depth", "dp", None), P("depth", "dp", None))
    body = functools.partial(shards, mesh.shape["depth"], mesh.shape["dp"])
    return jax.shard_map(body, mesh=mesh, in_specs=in_specs, out_specs=out_specs, check_vma=False)
```
